256 devices in a mesh: wide: 32 (over y_lo, z, core), narrow: 8 (over y_hi, x).
Axes of the slice: x: 4, y: 4 (y_hi: 2, y_lo: 2; y = y_hi * 2 + y_lo), z: 8, core: 2. Of those that a mesh axis runs over, the one named last changes fastest.
Arguments:
- compound_activation: bfloat16 [8, 5120, 2048], P('narrow', 'wide'), may hold values from -0.29882812 to 0.29882812
- compound_vectors: bfloat16 [8, 5120, 1024], P('narrow', 'wide'), may hold values from -2.34375 to 2.34375
- pathway_vectors: bfloat16 [8, 5120, 1024], P('narrow', 'wide'), may hold values from -2.34375 to 2.34375
- matching_pathway_index: int32 [8, 5120], P('narrow', 'wide'), may hold values from 0 to 5119, each once within a row
- exponent_of_sharpness: float32 [1], replicated, may hold values from 3.4 to 4.1
- offset_shift: float32 [1], replicated, may hold values from -4 to -2
- objective_seed: float32 [1], replicated, may hold values from 0.05 to 0.2
Outputs:
- weight_grad: float32 [2048, 1024], P('wide')
- route_grad: bfloat16 [8, 5120, 1024], P('narrow', 'wide')
The draws below stay inside these ranges and needn't reach their ends.
All inputs are finite; a program needn't handle non-finite values.
Results may differ from the reference program's by a relative error of at most 0.006.
Values may be sent and summed in bfloat16 or wider, within the bound.
A program may use at most 64 MiB of HBM per device.

```python
import math
import jax
import jax.numpy as jnp
from jax import lax

D = 1024
FF = 2048
GROUP = 5120
REPLICAS = 8


def scaled_rows(key, base):
    row_key, col_key = jax.random.split(key)
    row_scale = jnp.exp(jax.random.uniform(row_key, (REPLICAS, GROUP, 1), jnp.float32) * math.log(10.0))
    col_scale = jnp.exp(jax.random.uniform(col_key, (1, 1, D), jnp.float32) * math.log(10.0))
    values = base * row_scale * col_scale / (8.0 * math.sqrt(D))
    return values.astype(jnp.bfloat16)


def draw_compound_vectors(key, part):
    key = jax.random.fold_in(key, 11)
    base_key, scale_key = jax.random.split(key)
    base = jnp.clip(jax.random.normal(base_key, (REPLICAS, GROUP, D), jnp.float32), -6.0, 6.0)
    return scaled_rows(scale_key, base)


def draw_pathway_vectors(key, part):
    key = jax.random.fold_in(key, 23)
    base_key, scale_key = jax.random.split(key)
    base = jnp.clip(jax.random.normal(base_key, (REPLICAS, GROUP, D), jnp.float32), -6.0, 6.0)
    return scaled_rows(scale_key, base)


def raised(result, own_key, source, target, blocks, factor):
    def block_of(position):
        return (jnp.arange(result.shape[position]) // (result.shape[position] // blocks)).reshape((-1,) + (1,) * (result.ndim - 1 - position))

    near = jax.random.permutation(own_key, blocks)[block_of(target)]
    other_side = (block_of(target) + blocks // 2) % blocks
    return jnp.where((block_of(source) == near) | (block_of(source) == other_side), factor * result, result)


def level_of(own_key, shape, pieces, smallest, top_value):
    gain, own = 1.0, jax.random.fold_in(own_key, 6)
    for position, parts in pieces:
        steps = jnp.exp(jax.random.uniform(jax.random.fold_in(own, position), (parts,), jnp.float32, smallest / len(pieces), top_value / len(pieces)))
        gain = gain * jnp.repeat(steps, shape[position] // parts).reshape([-1 if axis == position else 1 for axis in range(len(shape))])
    return gain


def noise_with(stream_key, extent, scale, limit, cuts, heavy, kind=jnp.bfloat16):
    entries = scale * jax.random.normal(stream_key, extent, jnp.float32)
    if cuts:
        entries = entries * level_of(stream_key, extent, cuts, -0.22, 0.18)
    return jnp.clip(raised(entries, jax.random.fold_in(stream_key, 3), *heavy), -limit, limit).astype(kind)


def setup_inputs(seed: int = 0) -> dict:
    arg_keys = jax.random.split(jax.random.key(seed), 8)
    compound_activation = noise_with(arg_keys[0], (REPLICAS, GROUP, FF), 0.05, 0.29882812, ((0, 8), (1, 32)), (1, 2, 32, 2.75))
    compound_vectors = draw_compound_vectors(jax.random.fold_in(arg_keys[7], 71), 0)
    pathway_vectors = draw_pathway_vectors(jax.random.fold_in(arg_keys[7], 71), 0)
    matching_pathway_index = jax.vmap(lambda own: jax.random.permutation(own, GROUP))(jax.random.split(arg_keys[3], REPLICAS)).reshape((REPLICAS, GROUP)).astype(jnp.int32)
    exponent_of_sharpness = jnp.clip(jax.random.uniform(arg_keys[4], (1,), jnp.float32, 3.4, 4.1), 3.4, 4.1)
    offset_shift = jnp.clip(jax.random.uniform(arg_keys[5], (1,), jnp.float32, -4.0, -2.0), -4.0, -2.0)
    objective_seed = jnp.clip(jnp.exp(jax.random.uniform(arg_keys[6], (1,), jnp.float32, math.log(0.05), math.log(0.2))), 0.05, 0.2)
    return {"compound_activation": compound_activation, "compound_vectors": compound_vectors, "pathway_vectors": pathway_vectors, "matching_pathway_index": matching_pathway_index, "exponent_of_sharpness": exponent_of_sharpness, "offset_shift": offset_shift, "objective_seed": objective_seed}


def unit_rows(embed):
    values = embed.astype(jnp.float32)
    magnitude = jnp.sqrt(lax.optimization_barrier(jnp.sum(values * values, -1, keepdims=True)) + 1e-06)
    return (values / magnitude, magnitude)

def unit_back(unit_f, magnitude, upstream_grad):
    along = lax.optimization_barrier(jnp.sum(unit_f * upstream_grad, -1, keepdims=True))
    return (upstream_grad - unit_f * along) / magnitude

def reference(compound_activation, compound_vectors, pathway_vectors, matching_pathway_index, exponent_of_sharpness, offset_shift, objective_seed):
    score_sharpness = jnp.exp(exponent_of_sharpness[0])
    score_shift_amount = offset_shift[0]
    incoming_adjoint = objective_seed[0]

    def one_group(items):
        hidden, molecules, routes, targets = items
        mol_unit_f, mol_length = unit_rows(molecules)
        route_unit_f, route_length = unit_rows(routes)
        compound_normed_vectors = mol_unit_f.astype(jnp.bfloat16)
        pathway_normed_vectors = route_unit_f.astype(jnp.bfloat16)
        similarity_grid = jnp.dot(compound_normed_vectors, pathway_normed_vectors.T, preferred_element_type=jnp.float32)
        col_ids = jnp.arange(GROUP, dtype=jnp.int32)
        matching_mask = (col_ids[None, :] == targets[:, None]).astype(jnp.float32)
        derivative_parts = (incoming_adjoint * (jax.nn.sigmoid(score_sharpness * similarity_grid + score_shift_amount) - matching_mask)).astype(jnp.bfloat16)
        compound_normed_derivative = score_sharpness * jnp.dot(derivative_parts, pathway_normed_vectors, preferred_element_type=jnp.float32)
        pathway_normed_derivative = score_sharpness * jnp.dot(derivative_parts.T, compound_normed_vectors, preferred_element_type=jnp.float32)
        mol_dembed = unit_back(mol_unit_f, mol_length, compound_normed_derivative).astype(jnp.bfloat16)
        route_dembed = unit_back(route_unit_f, route_length, pathway_normed_derivative).astype(jnp.bfloat16)
        weight_term = jnp.dot(hidden.T, mol_dembed, preferred_element_type=jnp.float32)
        return (weight_term, route_dembed)
    weight_terms, route_grad = lax.map(one_group, (compound_activation, compound_vectors, pathway_vectors, matching_pathway_index))
    return (lax.optimization_barrier(jnp.sum(weight_terms, 0)), route_grad)
```

```python
import jax
import jax.numpy as jnp
from jax import lax
from jax.experimental import pallas as pl
from jax.experimental.pallas import tpu as pltpu
from jax.sharding import PartitionSpec as P

ROWS = 160
HALF = 80
D = 1024
FF = 2048
PAIR = 2 * ROWS
F32 = jnp.float32
BF16 = jnp.bfloat16
MESH = pl.DeviceIdType.MESH
NT = (((1,), (1,)), ((), ()))
NN = (((1,), (0,)), ((), ()))


def wide_of(y, z, c):
    return y * 16 + z * 2 + c


def wrap(i, n):
    return lax.rem(i + n, n)


def loop(n, body):
    lax.fori_loop(0, n, lambda i, _: (body(i), 0)[1], 0)


def kernel(
    act_ref,
    mol_ref,
    route_ref,
    target_ref,
    sharp_ref,
    shift_ref,
    seed_ref,
    weight_out,
    route_out,
    ring_r,
    ring_m,
    cross_m,
    cross_r,
    tring,
    tcross,
    tcol,
    part_m,
    part_r,
    sib_in,
    y_out,
    y_in,
    a_out,
    a_in,
    act_t,
    act_own,
    act_sib,
    mold,
    wsend,
    wrecv,
    zsend,
    zrecv,
    gath,
    ring_ss,
    ring_rs,
    cross_ss,
    cross_rs,
    t_ss,
    t_rs,
    red_ss,
    red_rs,
    mis_ss,
    mis_rs,
    w_ss,
    w_rs,
    z_ss,
    z_rs,
    g_ss,
    g_rs,
):
    w = lax.axis_index("wide")
    n = lax.axis_index("narrow")
    y = lax.div(w, 16)
    z = lax.rem(lax.div(w, 2), 8)
    c = lax.rem(w, 2)
    q = 2 * y + c
    e = y * 8 + n
    sib = (wide_of(y, z, 1 - c), n)
    across = (wide_of(1 - y, z, c), n)
    diag = (wide_of(1 - y, z, 1 - c), n)
    zpeer = [(wide_of(y, wrap(z + k, 8), c), n) for k in range(1, 8)]

    def w_index(r):
        return lax.rem(e + r + 16, 16)

    def w_peer(r):
        d = w_index(r)
        return (wide_of(lax.div(d, 8), z, c), lax.rem(d, 8))

    def n_peer(k):
        return (w, lax.rem(n + k, 8))

    barrier = pltpu.get_barrier_semaphore()
    partners = zpeer + [sib, diag] + [w_peer(r) for r in range(1, 16)]
    for dev in partners:
        pl.semaphore_signal(barrier, inc=1, device_id=dev, device_id_type=MESH)

    sent = []

    def remote(src, dst, ss, rs, dev):
        return pltpu.make_async_remote_copy(
            src_ref=src, dst_ref=dst, send_sem=ss, recv_sem=rs, device_id=dev, device_id_type=MESH
        )

    def send(*a):
        cp = remote(*a)
        cp.start()
        sent.append(cp)

    def block(q_):
        return pl.ds(pl.multiple_of(q_ * ROWS, ROWS), ROWS)

    def normalise(raw, ring, cross):
        def body(i):
            rows = pl.ds(pl.multiple_of(i * 32, 32), 32)
            v = raw[rows, :].astype(F32)
            inv = 1.0 / jnp.sqrt(jnp.sum(v * v, -1, keepdims=True) + 1e-06)
            u = (v * inv).astype(BF16)
            ring[z, rows, :] = u
            cross[pl.ds(pl.multiple_of(q * ROWS + i * 32, 32), 32), :] = u

        loop(ROWS // 32, body)

    normalise(route_ref, ring_r, cross_r)
    normalise(mol_ref, ring_m, cross_m)
    t_own = jnp.concatenate(
        [target_ref[...].astype(F32), jnp.zeros((1, 256 - ROWS), F32)], axis=1
    )
    t_own = jnp.broadcast_to(t_own, (8, 256))
    tring[z] = t_own
    tcross[q] = t_own

    pl.semaphore_wait(barrier, len(partners))

    rings = (ring_r, ring_m)

    def exists(d, k, h):
        return k < 3 or (k == 3 and h == d)

    def ring_copy(a, d, k, h, slot):
        i = ((a * 2 + d) * 4 + k) * 2 + h
        part = rings[a].at[slot, pl.ds(h * HALF, HALF)]
        dev = zpeer[0] if d == 0 else zpeer[6]
        return remote(part, part, ring_ss.at[i], ring_rs.at[i], dev)

    def ring_send(a, d, k, h):
        cp = ring_copy(a, d, k, h, wrap(z - k, 8) if d == 0 else wrap(z + k, 8))
        cp.start()
        sent.append(cp)

    def ring_wait(a, d, k, h):
        ring_copy(a, d, k, h, wrap(z - 1 - k, 8) if d == 0 else wrap(z + 1 + k, 8)).wait_recv()

    def advance(a, k, pieces=(0, 1)):
        for h in pieces:
            for d in (0, 1):
                if exists(d, k, h):
                    ring_wait(a, d, k, h)
                    if exists(d, k + 1, h):
                        ring_send(a, d, k + 1, h)

    def ring_open(a):
        for h in (0, 1):
            for d in (0, 1):
                ring_send(a, d, 0, h)

    crosses = (cross_m, cross_r)
    b_own, b_sib = block(q), block(2 * y + 1 - c)
    b_across, b_diag = block(2 * (1 - y) + c), block(2 * (1 - y) + 1 - c)

    def cross_copy(a, i, blk, dev):
        part = crosses[a].at[blk]
        return remote(part, part, cross_ss.at[a * 3 + i], cross_rs.at[a * 3 + i], dev)

    def cross_send(a, i):
        cp = cross_copy(a, i, b_across if i == 2 else b_own, across if i == 0 else sib)
        cp.start()
        sent.append(cp)

    def cross_wait(a, i):
        cross_copy(a, i, (b_across, b_sib, b_diag)[i], sib).wait_recv()

    for k in range(1, 8):
        send(tring.at[z], tring.at[z], t_ss.at[k - 1], t_rs.at[k - 1], zpeer[k - 1])
    for i, dev in enumerate((sib, across, diag)):
        send(tcross.at[q], tcross.at[q], t_ss.at[7 + i], t_rs.at[7 + i], dev)

    cross_send(0, 0)
    ring_open(0)
    cross_send(0, 1)

    for t in range(16):
        tile = act_ref[:, 128 * t : 128 * t + 128].astype(F32)
        act_t[128 * t : 128 * t + 128, :] = tile.T

    def order(j):
        yy, nn = lax.div(j, 8), lax.rem(j, 8)
        for h in (0, 1):
            parts = [
                act_t[pl.ds(pl.multiple_of(1024 * yy + 128 * zz + 64 * h + 8 * nn, 8), 8), :]
                for zz in range(8)
            ]
            act_own[h, pl.ds(pl.multiple_of(j * 64, 64), 64), :] = jnp.concatenate(
                parts, axis=0
            ).astype(BF16)

    loop(16, order)
    send(act_own.at[1 - c], act_sib, mis_ss.at[0], mis_rs.at[0], sib)

    advance(0, 0)
    cross_wait(0, 0)
    cross_send(0, 2)

    for k in range(1, 8):
        slot = wrap(z - k, 8)
        remote(
            tring.at[slot], tring.at[slot], t_ss.at[k - 1], t_rs.at[k - 1], sib
        ).wait_recv()
    for i, slot in enumerate((2 * y + 1 - c, 2 * (1 - y) + c, 2 * (1 - y) + 1 - c)):
        remote(
            tcross.at[slot], tcross.at[slot], t_ss.at[7 + i], t_rs.at[7 + i], sib
        ).wait_recv()
    eye = lax.broadcasted_iota(jnp.int32, (ROWS, ROWS), 0) == lax.broadcasted_iota(
        jnp.int32, (ROWS, ROWS), 1
    )
    for i in range(4):
        line = jnp.broadcast_to(tcross[i, 0:1, 0:ROWS], (ROWS, ROWS))
        col = jnp.sum(jnp.where(eye, line, 0.0), -1, keepdims=True)
        tcol[i * ROWS : (i + 1) * ROWS, :] = jnp.broadcast_to(col, (ROWS, 128))

    cross_wait(0, 1)
    cross_wait(0, 2)

    shift = shift_ref[0]
    seed = seed_ref[0]
    parts = (part_m, part_r)

    def pairs(a, slot, first):
        def body(b):
            rows = pl.ds(pl.multiple_of(b * PAIR, PAIR), PAIR)
            right = rings[a][slot]
            sharp = jnp.exp(jnp.full((1, ROWS), sharp_ref[0], F32))
            s = lax.dot_general(crosses[a][rows, :], right, NT, preferred_element_type=F32)
            if a == 0:
                base = wide_of(y, slot, c) * ROWS
                ids = lax.broadcasted_iota(jnp.int32, (1, ROWS), 1) + base
                match = tcol[rows, 0:1] == ids.astype(F32)
            else:
                base = wide_of(b, z, 0) * ROWS
                ids = lax.broadcasted_iota(jnp.int32, (PAIR, 1), 0) + base
                match = ids.astype(F32) == tring[slot, 0:1, 0:ROWS]
            g = jax.nn.sigmoid(s * sharp + shift) - jnp.where(match, 1.0, 0.0)
            g = (seed * g).astype(BF16)
            out = lax.dot_general(g, right, NN, preferred_element_type=F32)
            if first:
                parts[a][rows, :] = out
            else:
                parts[a][rows, :] += out

        loop(2, body)

    def pairs_at(a, k):
        loop(2, lambda i: pairs(a, wrap(z + (2 * i - 1) * k, 8), False))

    def reduce_open(a):
        send(parts[a].at[b_diag], sib_in.at[a, 0], red_ss.at[a * 4], red_rs.at[a * 4], sib)
        send(parts[a].at[b_sib], sib_in.at[a, 1], red_ss.at[a * 4 + 1], red_rs.at[a * 4 + 1], sib)

    def reduce_wait(a, i):
        dst = (sib_in.at[a, 0], sib_in.at[a, 1], y_in.at[a], a_in.at[a])[i]
        remote(dst, dst, red_ss.at[a * 4 + i], red_rs.at[a * 4 + i], sib).wait_recv()

    def reduce_across(a):
        reduce_wait(a, 0)

        def body(i):
            rows = pl.ds(pl.multiple_of(i * 32, 32), 32)
            far = pl.ds(pl.multiple_of((2 * (1 - y) + c) * ROWS + i * 32, 32), 32)
            total = parts[a][far, :] + sib_in[a, 0, rows, :]
            unit = crosses[a][far, :].astype(F32)
            along = jnp.sum(total * unit, -1, keepdims=True)
            y_out[a, rows, :] = (total - along * unit).astype(BF16)
            a_out[a, rows, :] = jnp.broadcast_to(along, (32, 128))

        loop(ROWS // 32, body)
        send(y_out.at[a], y_in.at[a], red_ss.at[a * 4 + 2], red_rs.at[a * 4 + 2], across)
        send(a_out.at[a], a_in.at[a], red_ss.at[a * 4 + 3], red_rs.at[a * 4 + 3], across)

    def reduce_close(a, raw, put):
        reduce_wait(a, 1)
        reduce_wait(a, 2)
        reduce_wait(a, 3)

        def body(i):
            rows = pl.ds(pl.multiple_of(i * 32, 32), 32)
            own = pl.ds(pl.multiple_of(q * ROWS + i * 32, 32), 32)
            sharp = jnp.exp(jnp.full((32, 1), sharp_ref[0], F32))
            total = parts[a][own, :] + sib_in[a, 1, rows, :] + y_in[a, rows, :].astype(F32)
            total = total + a_in[a, rows, 0:1] * crosses[a][own, :].astype(F32)
            v = raw[rows, :].astype(F32)
            inv = 1.0 / jnp.sqrt(jnp.sum(v * v, -1, keepdims=True) + 1e-06)
            unit = v * inv
            along = jnp.sum(unit * total, -1, keepdims=True)
            put(i, ((total - unit * along) * (inv * sharp)).astype(BF16))

        loop(ROWS // 32, body)

    pairs(0, z, True)
    pairs_at(0, 1)
    advance(0, 1)
    cross_send(1, 0)
    cross_send(1, 1)
    pairs_at(0, 2)
    advance(0, 2)
    ring_open(1)
    pairs_at(0, 3)
    cross_wait(1, 0)
    cross_send(1, 2)
    advance(0, 3)
    pairs(0, wrap(z + 4, 8), False)

    reduce_open(0)
    advance(1, 0, (0,))
    reduce_across(0)
    cross_wait(1, 1)
    cross_wait(1, 2)
    pairs(1, z, True)
    advance(1, 0, (1,))
    pairs_at(1, 1)
    advance(1, 1, (0,))

    def put_mold(i, value):
        mold[c, pl.ds(pl.multiple_of(i * 32, 32), 32), :] = value

    reduce_close(0, mol_ref, put_mold)
    send(mold.at[c], mold.at[c], mis_ss.at[1], mis_rs.at[1], sib)
    advance(1, 1, (1,))
    remote(act_sib, act_sib, mis_ss.at[0], mis_rs.at[0], sib).wait_recv()
    remote(mold.at[1 - c], mold.at[1 - c], mis_ss.at[1], mis_rs.at[1], sib).wait_recv()

    def weight(i):
        cols = pl.ds(pl.multiple_of(i * 256, 256), 256)
        prod = lax.dot_general(act_own[c], mold[c, :, cols], NN, preferred_element_type=F32)
        prod += lax.dot_general(act_sib[...], mold[1 - c, :, cols], NN, preferred_element_type=F32)
        wsend[:, :, cols] = prod.astype(BF16).reshape(16, 64, 256)

    loop(4, weight)
    for r in range(1, 16):
        send(wsend.at[w_index(r)], wrecv.at[e], w_ss.at[r - 1], w_rs.at[r - 1], w_peer(r))

    advance(1, 2, (0,))
    pairs_at(1, 2)
    advance(1, 2, (1,))
    pairs_at(1, 3)
    advance(1, 3)
    pairs(1, wrap(z + 4, 8), False)
    reduce_open(1)
    reduce_across(1)

    for r in range(1, 16):
        slot = w_index(-r)
        remote(
            wrecv.at[slot], wrecv.at[slot], w_ss.at[r - 1], w_rs.at[r - 1], sib
        ).wait_recv()

    def gather_sum(i):
        rows = pl.ds(pl.multiple_of(i * 16, 16), 16)
        total = wsend[e, rows, :].astype(F32)
        for r in range(1, 16):
            total += wrecv[w_index(-r), rows, :].astype(F32)
        zsend[rows, :] = total

    loop(4, gather_sum)
    for k in range(1, 8):
        src = zsend.at[pl.ds(pl.multiple_of(wrap(z + k, 8) * 8, 8), 8)]
        send(src, zrecv.at[z], z_ss.at[k - 1], z_rs.at[k - 1], zpeer[k - 1])

    def put_route(i, value):
        route_out[pl.ds(pl.multiple_of(i * 32, 32), 32), :] = value

    reduce_close(1, route_ref, put_route)

    total = zsend[pl.ds(pl.multiple_of(z * 8, 8), 8), :]
    for k in range(1, 8):
        slot = wrap(z - k, 8)
        remote(
            zrecv.at[slot], zrecv.at[slot], z_ss.at[k - 1], z_rs.at[k - 1], sib
        ).wait_recv()
        total += zrecv[slot]
    gath[n] = total
    for k in range(1, 8):
        send(gath.at[n], gath.at[n], g_ss.at[k - 1], g_rs.at[k - 1], n_peer(k))
    for k in range(1, 8):
        slot = wrap(n - k, 8)
        remote(
            gath.at[slot], gath.at[slot], g_ss.at[k - 1], g_rs.at[k - 1], sib
        ).wait_recv()
    weight_out[...] = gath[...].reshape(64, D)
    for cp in sent:
        cp.wait_send()


def local(
    compound_activation,
    compound_vectors,
    pathway_vectors,
    matching_pathway_index,
    exponent_of_sharpness,
    offset_shift,
    objective_seed,
):
    vmem = pl.BlockSpec(memory_space=pltpu.VMEM)
    smem = pl.BlockSpec(memory_space=pltpu.SMEM)
    dma = pltpu.SemaphoreType.DMA
    weight_grad, route_grad = pl.pallas_call(
        kernel,
        out_shape=(
            jax.ShapeDtypeStruct((64, D), F32),
            jax.ShapeDtypeStruct((ROWS, D), BF16),
        ),
        in_specs=[vmem] * 4 + [smem] * 3,
        out_specs=(vmem, vmem),
        scratch_shapes=[
            pltpu.VMEM((8, ROWS, D), BF16),
            pltpu.VMEM((8, ROWS, D), BF16),
            pltpu.VMEM((4 * ROWS, D), BF16),
            pltpu.VMEM((4 * ROWS, D), BF16),
            pltpu.VMEM((8, 8, 256), F32),
            pltpu.VMEM((4, 8, 256), F32),
            pltpu.VMEM((4 * ROWS, 128), F32),
            pltpu.VMEM((4 * ROWS, D), F32),
            pltpu.VMEM((4 * ROWS, D), F32),
            pltpu.VMEM((2, 2, ROWS, D), F32),
            pltpu.VMEM((2, ROWS, D), BF16),
            pltpu.VMEM((2, ROWS, D), BF16),
            pltpu.VMEM((2, ROWS, 128), F32),
            pltpu.VMEM((2, ROWS, 128), F32),
            pltpu.VMEM((FF, ROWS), F32),
            pltpu.VMEM((2, FF // 2, ROWS), BF16),
            pltpu.VMEM((FF // 2, ROWS), BF16),
            pltpu.VMEM((2, ROWS, D), BF16),
            pltpu.VMEM((16, 64, D), BF16),
            pltpu.VMEM((16, 64, D), BF16),
            pltpu.VMEM((64, D), F32),
            pltpu.VMEM((8, 8, D), F32),
            pltpu.VMEM((8, 8, D), F32),
            dma((32,)),
            dma((32,)),
            dma((6,)),
            dma((6,)),
            dma((10,)),
            dma((10,)),
            dma((8,)),
            dma((8,)),
            dma((2,)),
            dma((2,)),
            dma((15,)),
            dma((15,)),
            dma((7,)),
            dma((7,)),
            dma((7,)),
            dma((7,)),
        ],
        compiler_params=pltpu.CompilerParams(
            collective_id=0, has_side_effects=True, vmem_limit_bytes=48 * 1024 * 1024
        ),
        name="contrastive_backward",
    )(
        compound_activation[0],
        compound_vectors[0],
        pathway_vectors[0],
        matching_pathway_index,
        exponent_of_sharpness,
        offset_shift,
        objective_seed,
    )
    return weight_grad, route_grad[None]


def solution(mesh):
    in_specs = (
        P("narrow", "wide", None),
        P("narrow", "wide", None),
        P("narrow", "wide", None),
        P("narrow", "wide"),
        P(),
        P(),
        P(),
    )
    out_specs = (P("wide", None), P("narrow", "wide", None))
    return jax.shard_map(local, mesh=mesh, in_specs=in_specs, out_specs=out_specs, check_vma=False)
```

```python
import jax
import jax.numpy as jnp
from jax import lax
from jax.experimental import pallas as pl
from jax.experimental.pallas import tpu as pltpu
from jax.sharding import PartitionSpec as P

ROWS = 160
HALF = 80
D = 1024
FF = 2048
PAIR = 2 * ROWS
F32 = jnp.float32
BF16 = jnp.bfloat16
MESH = pl.DeviceIdType.MESH
NT = (((1,), (1,)), ((), ()))
NN = (((1,), (0,)), ((), ()))


def wide_of(y, z, c):
    return y * 16 + z * 2 + c


def wrap(i, n):
    return lax.rem(i + n, n)


def loop(n, body):
    lax.fori_loop(0, n, lambda i, _: (body(i), 0)[1], 0)


def kernel(
    act_hbm,
    mol_hbm,
    route_hbm,
    target_ref,
    sharp_ref,
    shift_ref,
    seed_ref,
    weight_out,
    route_out,
    act_ref,
    mol_ref,
    route_ref,
    ring_r,
    ring_m,
    cross_m,
    cross_r,
    tring,
    tcross,
    tcol,
    part_m,
    part_r,
    sib_in,
    y_out,
    y_in,
    a_out,
    a_in,
    act_t,
    act_own,
    act_x,
    act_y,
    mold_x,
    mold_y,
    prod,
    wsend,
    wrecv,
    zown,
    zsend,
    zrecv,
    gath,
    ring_ss,
    ring_rs,
    cross_ss,
    cross_rs,
    t_ss,
    t_rs,
    red_ss,
    red_rs,
    in_s,
    act_ss,
    act_rs,
    mold_ss,
    mold_rs,
    w_ss,
    w_rs,
    z_ss,
    z_rs,
    g_ss,
    g_rs,
):
    w = lax.axis_index("wide")
    n = lax.axis_index("narrow")
    y = lax.div(w, 16)
    z = lax.rem(lax.div(w, 2), 8)
    c = lax.rem(w, 2)
    q = 2 * y + c
    e = y * 8 + n
    sib = (wide_of(y, z, 1 - c), n)
    across = (wide_of(1 - y, z, c), n)
    diag = (wide_of(1 - y, z, 1 - c), n)
    zpeer = [(wide_of(y, wrap(z + k, 8), c), n) for k in range(1, 8)]

    x = lax.rem(n, 4)
    yh = lax.div(n, 4)
    v = 2 * y + yh

    def x_peer(k, cc):
        return (wide_of(y, z, cc), yh * 4 + wrap(x + k, 4))

    def y_peer(k, cc):
        far = wrap(v + k, 4)
        return (wide_of(lax.div(far, 2), z, cc), lax.rem(far, 2) * 4 + x)

    line_peer = (x_peer, y_peer)
    line_at = (x, v)

    loads = [
        pltpu.make_async_copy(src, dst, in_s.at[i])
        for i, (src, dst) in enumerate(
            ((route_hbm, route_ref), (mol_hbm, mol_ref), (act_hbm, act_ref))
        )
    ]
    for cp in loads:
        cp.start()

    barrier = pltpu.get_barrier_semaphore()
    partners = zpeer + [sib]
    for peer in line_peer:
        partners += [peer(k, cc) for k in (1, 2, 3) for cc in (c, 1 - c)]
    for k in (1, 2, 3):
        partners.append((w, (1 - yh) * 4 + wrap(x + k, 4)))
    for dev in partners:
        pl.semaphore_signal(barrier, inc=1, device_id=dev, device_id_type=MESH)

    sent = []

    def remote(src, dst, ss, rs, dev):
        return pltpu.make_async_remote_copy(
            src_ref=src, dst_ref=dst, send_sem=ss, recv_sem=rs, device_id=dev, device_id_type=MESH
        )

    def send(*a):
        cp = remote(*a)
        cp.start()
        sent.append(cp)

    def block(q_):
        return pl.ds(pl.multiple_of(q_ * ROWS, ROWS), ROWS)

    def normalise(raw, ring, cross):
        def body(i):
            rows = pl.ds(pl.multiple_of(i * 32, 32), 32)
            v = raw[rows, :].astype(F32)
            inv = 1.0 / jnp.sqrt(jnp.sum(v * v, -1, keepdims=True) + 1e-06)
            u = (v * inv).astype(BF16)
            ring[z, rows, :] = u
            cross[pl.ds(pl.multiple_of(q * ROWS + i * 32, 32), 32), :] = u

        loop(ROWS // 32, body)

    loads[0].wait()
    normalise(route_ref, ring_r, cross_r)
    loads[1].wait()
    normalise(mol_ref, ring_m, cross_m)
    t_own = jnp.concatenate(
        [target_ref[...].astype(F32), jnp.zeros((1, 256 - ROWS), F32)], axis=1
    )
    t_own = jnp.broadcast_to(t_own, (8, 256))
    tring[z] = t_own
    tcross[q] = t_own

    pl.semaphore_wait(barrier, len(partners))

    rings = (ring_r, ring_m)

    def exists(d, k, h):
        return k < 3 or (k == 3 and h == d)

    def ring_copy(a, d, k, h, slot):
        i = ((a * 2 + d) * 4 + k) * 2 + h
        part = rings[a].at[slot, pl.ds(h * HALF, HALF)]
        dev = zpeer[0] if d == 0 else zpeer[6]
        return remote(part, part, ring_ss.at[i], ring_rs.at[i], dev)

    def ring_send(a, d, k, h):
        cp = ring_copy(a, d, k, h, wrap(z - k, 8) if d == 0 else wrap(z + k, 8))
        cp.start()
        sent.append(cp)

    def ring_wait(a, d, k, h):
        ring_copy(a, d, k, h, wrap(z - 1 - k, 8) if d == 0 else wrap(z + 1 + k, 8)).wait_recv()

    def advance(a, k, pieces=(0, 1)):
        for h in pieces:
            for d in (0, 1):
                if exists(d, k, h):
                    ring_wait(a, d, k, h)
                    if exists(d, k + 1, h):
                        ring_send(a, d, k + 1, h)

    def ring_open(a):
        for h in (0, 1):
            for d in (0, 1):
                ring_send(a, d, 0, h)

    crosses = (cross_m, cross_r)
    b_own, b_sib = block(q), block(2 * y + 1 - c)
    b_across, b_diag = block(2 * (1 - y) + c), block(2 * (1 - y) + 1 - c)

    def cross_copy(a, i, blk, dev):
        part = crosses[a].at[blk]
        return remote(part, part, cross_ss.at[a * 3 + i], cross_rs.at[a * 3 + i], dev)

    def cross_send(a, i):
        cp = cross_copy(a, i, b_across if i == 2 else b_own, across if i == 0 else sib)
        cp.start()
        sent.append(cp)

    def cross_wait(a, i):
        cross_copy(a, i, (b_across, b_sib, b_diag)[i], sib).wait_recv()

    def target_ring():
        for k in range(1, 8):
            send(tring.at[z], tring.at[z], t_ss.at[k - 1], t_rs.at[k - 1], zpeer[k - 1])

    def target_ring_wait():
        for k in range(1, 8):
            at = tring.at[wrap(z - k, 8)]
            remote(at, at, t_ss.at[k - 1], t_rs.at[k - 1], sib).wait_recv()

    ring_open(0)
    cross_send(0, 0)
    for i, dev in enumerate((across, sib, diag)):
        send(tcross.at[q], tcross.at[q], t_ss.at[7 + i], t_rs.at[7 + i], dev)
    cross_send(0, 1)

    loads[2].wait()
    for t in range(16):
        tile = act_ref[:, 128 * t : 128 * t + 128].astype(F32)
        act_t[128 * t : 128 * t + 128, :] = tile.T

    def order(j):
        vv, xx = lax.div(j, 4), lax.rem(j, 4)
        yy, nn = lax.div(vv, 2), lax.rem(vv, 2) * 4 + xx
        for h in (0, 1):
            rows = [
                act_t[pl.ds(pl.multiple_of(1024 * yy + 128 * zz + 64 * h + 8 * nn, 8), 8), :]
                for zz in range(8)
            ]
            act_own[h, vv, xx] = jnp.concatenate(rows, axis=0).astype(BF16)

    loop(16, order)

    acts = (act_x, act_y)
    molds = (mold_x, mold_y)

    def act_part(l, h, at):
        return act_own.at[h, :, at] if l == 0 else act_own.at[h, at]

    own_acts = [
        pltpu.make_async_copy(act_part(l, c, line_at[l]), acts[l].at[line_at[l], c], in_s.at[3 + l])
        for l in (0, 1)
    ]
    for cp in own_acts:
        cp.start()

    def act_send(l):
        here = acts[l].at[line_at[l], c]
        for k in range(4):
            for o in (0, 1):
                if k + o > 0:
                    i = l * 8 + k * 2 + o
                    cc = c if o == 0 else 1 - c
                    src = act_part(l, cc, wrap(line_at[l] + k, 4))
                    send(src, here, act_ss.at[i], act_rs.at[i], line_peer[l](k, cc))

    def act_wait():
        for cp in own_acts:
            cp.wait()
        for l in (0, 1):
            for k in range(4):
                for o in (0, 1):
                    if k + o > 0:
                        i = l * 8 + k * 2 + o
                        cc = c if o == 0 else 1 - c
                        dst = acts[l].at[wrap(line_at[l] - k, 4), cc]
                        remote(dst, dst, act_ss.at[i], act_rs.at[i], sib).wait_recv()

    def mold_copy(l, k, o, at, dev):
        i = l * 8 + k * 2 + o
        return remote(at, at, mold_ss.at[i], mold_rs.at[i], dev)

    def mold_send(l, k, o):
        if o == 0:
            at, dev = molds[l].at[line_at[l], c], line_peer[l](k, c)
        else:
            at, dev = molds[l].at[wrap(line_at[l] - k, 4), c], sib
        cp = mold_copy(l, k, o, at, dev)
        cp.start()
        sent.append(cp)

    def mold_wait(l, k, o):
        at = molds[l].at[wrap(line_at[l] - k, 4), c if o == 0 else 1 - c]
        mold_copy(l, k, o, at, sib).wait_recv()

    advance(0, 0)
    cross_wait(0, 0)
    cross_send(0, 2)

    for i, slot in enumerate((2 * (1 - y) + c, 2 * y + 1 - c, 2 * (1 - y) + 1 - c)):
        remote(
            tcross.at[slot], tcross.at[slot], t_ss.at[7 + i], t_rs.at[7 + i], sib
        ).wait_recv()
    eye = lax.broadcasted_iota(jnp.int32, (ROWS, ROWS), 0) == lax.broadcasted_iota(
        jnp.int32, (ROWS, ROWS), 1
    )
    for i in range(4):
        line = jnp.broadcast_to(tcross[i, 0:1, 0:ROWS], (ROWS, ROWS))
        col = jnp.sum(jnp.where(eye, line, 0.0), -1, keepdims=True)
        tcol[i * ROWS : (i + 1) * ROWS, :] = jnp.broadcast_to(col, (ROWS, 128))

    cross_wait(0, 1)
    cross_wait(0, 2)

    shift = shift_ref[0]
    seed = seed_ref[0]
    parts = (part_m, part_r)

    def pairs(a, slot, first=False):
        right = rings[a][slot]
        sharp = jnp.exp(jnp.full((1, ROWS), sharp_ref[0], F32))
        blocks = [pl.ds(i * ROWS, ROWS) for i in range(4)]

        def grads(i, s):
            if a == 0:
                ids = lax.broadcasted_iota(jnp.int32, (1, ROWS), 1) + wide_of(y, slot, c) * ROWS
                match = tcol[blocks[i], 0:1] == ids.astype(F32)
            else:
                base = wide_of(i // 2, z, i % 2) * ROWS
                ids = lax.broadcasted_iota(jnp.int32, (ROWS, 1), 0) + base
                match = ids.astype(F32) == tring[slot, 0:1, 0:ROWS]
            g = jax.nn.sigmoid(s * sharp + shift) - jnp.where(match, 1.0, 0.0)
            return (seed * g).astype(BF16)

        scores = [
            lax.dot_general(crosses[a][b, :], right, NT, preferred_element_type=F32)
            for b in blocks
        ]
        gs = [grads(i, s) for i, s in enumerate(scores)]
        for b, g in zip(blocks, gs):
            out = lax.dot_general(g, right, NN, preferred_element_type=F32)
            if first:
                parts[a][b, :] = out
            else:
                parts[a][b, :] += out

    def pairs_left(a, k):
        pairs(a, wrap(z - k, 8))

    def pairs_right(a, k):
        pairs(a, wrap(z + k, 8))

    def pairs_at(a, k):
        loop(2, lambda i: pairs(a, wrap(z + (2 * i - 1) * k, 8)))

    def reduce_open(a):
        send(parts[a].at[b_diag], sib_in.at[a, 0], red_ss.at[a * 4], red_rs.at[a * 4], sib)
        send(parts[a].at[b_sib], sib_in.at[a, 1], red_ss.at[a * 4 + 1], red_rs.at[a * 4 + 1], sib)

    def reduce_wait(a, i):
        dst = (sib_in.at[a, 0], sib_in.at[a, 1], y_in.at[a], a_in.at[a])[i]
        remote(dst, dst, red_ss.at[a * 4 + i], red_rs.at[a * 4 + i], sib).wait_recv()

    def diagonal(i):
        row = lax.broadcasted_iota(jnp.int32, (32, ROWS), 0) + i * 32
        return row == lax.broadcasted_iota(jnp.int32, (32, ROWS), 1)

    def reduce_across(a):
        a_out[a] = jnp.zeros((8, ROWS), F32)
        reduce_wait(a, 0)

        def body(i):
            rows = pl.ds(pl.multiple_of(i * 32, 32), 32)
            far = pl.ds(pl.multiple_of((2 * (1 - y) + c) * ROWS + i * 32, 32), 32)
            total = parts[a][far, :] + sib_in[a, 0, rows, :]
            unit = crosses[a][far, :].astype(F32)
            along = jnp.sum(total * unit, -1, keepdims=True)
            y_out[a, rows, :] = (total - along * unit).astype(BF16)
            spread = jnp.sum(jnp.where(diagonal(i), along, 0.0), 0, keepdims=True)
            a_out[a] += jnp.broadcast_to(spread, (8, ROWS))

        loop(ROWS // 32, body)
        send(y_out.at[a], y_in.at[a], red_ss.at[a * 4 + 2], red_rs.at[a * 4 + 2], across)
        send(a_out.at[a], a_in.at[a], red_ss.at[a * 4 + 3], red_rs.at[a * 4 + 3], across)

    def reduce_close(a, raw, put):
        reduce_wait(a, 1)
        reduce_wait(a, 2)
        reduce_wait(a, 3)

        def body(i):
            rows = pl.ds(pl.multiple_of(i * 32, 32), 32)
            own = pl.ds(pl.multiple_of(q * ROWS + i * 32, 32), 32)
            sharp = jnp.exp(jnp.full((32, 1), sharp_ref[0], F32))
            total = parts[a][own, :] + sib_in[a, 1, rows, :] + y_in[a, rows, :].astype(F32)
            along = jnp.sum(jnp.where(diagonal(i), a_in[a, 0:1, :], 0.0), -1, keepdims=True)
            total = total + along * crosses[a][own, :].astype(F32)
            v = raw[rows, :].astype(F32)
            inv = 1.0 / jnp.sqrt(jnp.sum(v * v, -1, keepdims=True) + 1e-06)
            unit = v * inv
            along = jnp.sum(unit * total, -1, keepdims=True)
            put(i, ((total - unit * along) * (inv * sharp)).astype(BF16))

        loop(ROWS // 32, body)

    cross_send(1, 0)
    cross_send(1, 1)
    target_ring()
    act_send(0)
    act_send(1)
    pairs(0, z, True)
    pairs_left(0, 1)
    advance(0, 1, (0,))
    pairs_right(0, 1)
    advance(0, 1, (1,))
    pairs_left(0, 2)
    advance(0, 2, (0,))
    pairs_right(0, 2)
    advance(0, 2, (1,))
    ring_open(1)
    cross_wait(1, 0)
    cross_send(1, 2)
    pairs_at(0, 3)
    advance(0, 3)
    pairs_right(0, 4)

    reduce_open(0)
    cross_wait(1, 1)
    cross_wait(1, 2)
    target_ring_wait()
    advance(1, 0, (0,))
    reduce_across(0)
    pairs(1, z, True)
    advance(1, 0, (1,))
    pairs_left(1, 1)
    advance(1, 1, (0,))
    pairs_right(1, 1)
    advance(1, 1, (1,))

    def put_mold(i, value):
        rows = pl.ds(pl.multiple_of(i * 32, 32), 32)
        mold_x[x, c, rows, :] = value[:, : D // 2]
        mold_y[v, c, rows, :] = value[:, D // 2 :]

    reduce_close(0, mol_ref, put_mold)
    for k in (2, 1, 3):
        for l in (0, 1):
            mold_send(l, k, 0)
    for l in (0, 1):
        mold_send(l, 0, 1)
    pairs_left(1, 2)
    advance(1, 2, (0,))
    pairs_right(1, 2)
    advance(1, 2, (1,))
    for k in (1, 3, 2):
        for l in (0, 1):
            mold_wait(l, k, 0)
            mold_send(l, k, 1)
    pairs_left(1, 3)
    act_wait()
    for k in (0, 1, 3, 2):
        for l in (0, 1):
            mold_wait(l, k, 1)

    def weight(i):
        cols = pl.ds(pl.multiple_of(i * 256, 256), 256)
        for l in (0, 1):
            total = jnp.zeros((256, 256), F32)
            for p in range(4):
                for cc in (0, 1):
                    total += lax.dot_general(
                        acts[l][p, cc].reshape(256, ROWS),
                        molds[l][p, cc, :, cols],
                        NN,
                        preferred_element_type=F32,
                    )
            total = total.reshape(4, 64, 256)
            prod[l, :, :, cols] = total
            wsend[l, :, :, cols] = total.astype(BF16)

    loop(2, weight)
    for k in (2, 1, 3):
        for l in (0, 1):
            m = 1 - l
            i = l * 3 + k - 1
            src = wsend.at[l, wrap(line_at[m] + k, 4)]
            send(src, wrecv.at[l, line_at[m]], w_ss.at[i], w_rs.at[i], line_peer[m](k, c))

    pairs_right(1, 3)
    advance(1, 3)
    pairs_right(1, 4)
    reduce_open(1)
    reduce_across(1)

    for l in (0, 1):
        for k in (1, 2, 3):
            i = l * 3 + k - 1
            at = wrecv.at[l, wrap(line_at[1 - l] - k, 4)]
            remote(at, at, w_ss.at[i], w_rs.at[i], sib).wait_recv()

    def gather_sum(i):
        rows = pl.ds(pl.multiple_of(i * 16, 16), 16)
        halves = []
        for l in (0, 1):
            total = prod[l, line_at[1 - l], rows, :]
            for k in (1, 2, 3):
                total += wrecv[l, wrap(line_at[1 - l] - k, 4), rows, :].astype(F32)
            halves.append(total)
        for o in (0, 1):
            both = jnp.concatenate([total[8 * o : 8 * o + 8, :] for total in halves], axis=0)
            zown[2 * i + o] = both
            zsend[2 * i + o] = both.astype(BF16)

    loop(4, gather_sum)
    for k in range(1, 8):
        src = zsend.at[wrap(z + k, 8)]
        send(src, zrecv.at[z], z_ss.at[k - 1], z_rs.at[k - 1], zpeer[k - 1])
    total = zown[z]
    for k in range(1, 8):
        at = zrecv.at[wrap(z - k, 8)]
        remote(at, at, z_ss.at[k - 1], z_rs.at[k - 1], sib).wait_recv()
        total += zrecv[wrap(z - k, 8)].astype(F32)
    total = jnp.concatenate([total[0:8, :], total[8:16, :]], axis=1)
    gath[n] = total
    for k in (4, 2, 6, 1, 3, 5, 7):
        dev = (w, lax.rem(n + k, 8))
        send(gath.at[n], gath.at[n], g_ss.at[k - 1], g_rs.at[k - 1], dev)

    def put_route(i, value):
        route_out[pl.ds(pl.multiple_of(i * 32, 32), 32), :] = value

    reduce_close(1, route_ref, put_route)
    for k in range(1, 8):
        at = gath.at[lax.rem(n - k + 8, 8)]
        remote(at, at, g_ss.at[k - 1], g_rs.at[k - 1], sib).wait_recv()
    weight_out[...] = gath[...].reshape(64, D)
    for cp in sent:
        cp.wait_send()


def local(
    compound_activation,
    compound_vectors,
    pathway_vectors,
    matching_pathway_index,
    exponent_of_sharpness,
    offset_shift,
    objective_seed,
):
    vmem = pl.BlockSpec(memory_space=pltpu.VMEM)
    hbm = pl.BlockSpec(memory_space=pltpu.HBM)
    smem = pl.BlockSpec(memory_space=pltpu.SMEM)
    dma = pltpu.SemaphoreType.DMA
    weight_grad, route_grad = pl.pallas_call(
        kernel,
        out_shape=(
            jax.ShapeDtypeStruct((64, D), F32),
            jax.ShapeDtypeStruct((ROWS, D), BF16),
        ),
        in_specs=[hbm] * 3 + [vmem] + [smem] * 3,
        out_specs=(vmem, vmem),
        scratch_shapes=[
            pltpu.VMEM((ROWS, FF), BF16),
            pltpu.VMEM((ROWS, D), BF16),
            pltpu.VMEM((ROWS, D), BF16),
            pltpu.VMEM((8, ROWS, D), BF16),
            pltpu.VMEM((8, ROWS, D), BF16),
            pltpu.VMEM((4 * ROWS, D), BF16),
            pltpu.VMEM((4 * ROWS, D), BF16),
            pltpu.VMEM((8, 8, 256), F32),
            pltpu.VMEM((4, 8, 256), F32),
            pltpu.VMEM((4 * ROWS, 128), F32),
            pltpu.VMEM((4 * ROWS, D), F32),
            pltpu.VMEM((4 * ROWS, D), F32),
            pltpu.VMEM((2, 2, ROWS, D), F32),
            pltpu.VMEM((2, ROWS, D), BF16),
            pltpu.VMEM((2, ROWS, D), BF16),
            pltpu.VMEM((2, 8, ROWS), F32),
            pltpu.VMEM((2, 8, ROWS), F32),
            pltpu.VMEM((FF, ROWS), F32),
            pltpu.VMEM((2, 4, 4, 64, ROWS), BF16),
            pltpu.VMEM((4, 2, 4, 64, ROWS), BF16),
            pltpu.VMEM((4, 2, 4, 64, ROWS), BF16),
            pltpu.VMEM((4, 2, ROWS, D // 2), BF16),
            pltpu.VMEM((4, 2, ROWS, D // 2), BF16),
            pltpu.VMEM((2, 4, 64, D // 2), F32),
            pltpu.VMEM((2, 4, 64, D // 2), BF16),
            pltpu.VMEM((2, 4, 64, D // 2), BF16),
            pltpu.VMEM((8, 16, D // 2), F32),
            pltpu.VMEM((8, 16, D // 2), BF16),
            pltpu.VMEM((8, 16, D // 2), BF16),
            pltpu.VMEM((8, 8, D), F32),
            dma((32,)),
            dma((32,)),
            dma((6,)),
            dma((6,)),
            dma((10,)),
            dma((10,)),
            dma((8,)),
            dma((8,)),
            dma((5,)),
            dma((16,)),
            dma((16,)),
            dma((16,)),
            dma((16,)),
            dma((6,)),
            dma((6,)),
            dma((7,)),
            dma((7,)),
            dma((7,)),
            dma((7,)),
        ],
        compiler_params=pltpu.CompilerParams(
            collective_id=0, has_side_effects=True, vmem_limit_bytes=60 * 1024 * 1024
        ),
        name="contrastive_backward",
    )(
        compound_activation[0],
        compound_vectors[0],
        pathway_vectors[0],
        matching_pathway_index,
        exponent_of_sharpness,
        offset_shift,
        objective_seed,
    )
    return weight_grad, route_grad[None]


def solution(mesh):
    in_specs = (
        P("narrow", "wide", None),
        P("narrow", "wide", None),
        P("narrow", "wide", None),
        P("narrow", "wide"),
        P(),
        P(),
        P(),
    )
    out_specs = (P("wide", None), P("narrow", "wide", None))
    return jax.shard_map(local, mesh=mesh, in_specs=in_specs, out_specs=out_specs, check_vma=False)
```

```python
import jax
import jax.numpy as jnp
from jax import lax
from jax.experimental import pallas as pl
from jax.experimental.pallas import tpu as pltpu
from jax.sharding import PartitionSpec as P

ROWS = 160
PIECES = ((0, 48), (48, 32), (80, 48), (128, 32))
CHUNKS = ((0, 64), (64, 96))
D = 1024
FF = 2048
PAIR = 2 * ROWS
F32 = jnp.float32
BF16 = jnp.bfloat16
MESH = pl.DeviceIdType.MESH
NT = (((1,), (1,)), ((), ()))
NN = (((1,), (0,)), ((), ()))


def wide_of(y, z, c):
    return y * 16 + z * 2 + c


def wrap(i, n):
    return lax.rem(i + n, n)


def loop(n, body):
    lax.fori_loop(0, n, lambda i, _: (body(i), 0)[1], 0)


def kernel(
    act_hbm,
    mol_hbm,
    route_hbm,
    target_ref,
    sharp_ref,
    shift_ref,
    seed_ref,
    weight_out,
    route_out,
    act_ref,
    mol_ref,
    route_ref,
    ring_r,
    ring_m,
    cross_m,
    cross_r,
    tring,
    tcross,
    tcol,
    part_m,
    part_r,
    sib_in,
    y_out,
    y_in,
    a_out,
    a_in,
    act_t,
    act_own,
    act_x,
    act_y,
    mold_x,
    mold_y,
    prod,
    wsend,
    wrecv,
    zown,
    zsend,
    zrecv,
    gath,
    ring_ss,
    ring_rs,
    cross_ss,
    cross_rs,
    t_ss,
    t_rs,
    red_ss,
    red_rs,
    in_s,
    act_ss,
    act_rs,
    mold_ss,
    mold_rs,
    w_ss,
    w_rs,
    z_ss,
    z_rs,
    g_ss,
    g_rs,
):
    w = lax.axis_index("wide")
    n = lax.axis_index("narrow")
    y = lax.div(w, 16)
    z = lax.rem(lax.div(w, 2), 8)
    c = lax.rem(w, 2)
    q = 2 * y + c
    e = y * 8 + n
    sib = (wide_of(y, z, 1 - c), n)
    across = (wide_of(1 - y, z, c), n)
    diag = (wide_of(1 - y, z, 1 - c), n)
    zpeer = [(wide_of(y, wrap(z + k, 8), c), n) for k in range(1, 8)]

    x = lax.rem(n, 4)
    yh = lax.div(n, 4)
    v = 2 * y + yh

    def x_peer(k, cc):
        return (wide_of(y, z, cc), yh * 4 + wrap(x + k, 4))

    def y_peer(k, cc):
        far = wrap(v + k, 4)
        return (wide_of(lax.div(far, 2), z, cc), lax.rem(far, 2) * 4 + x)

    line_peer = (x_peer, y_peer)
    line_at = (x, v)

    loads = [
        pltpu.make_async_copy(src, dst, in_s.at[i])
        for i, (src, dst) in enumerate(
            ((route_hbm, route_ref), (mol_hbm, mol_ref), (act_hbm, act_ref))
        )
    ]
    for cp in loads:
        cp.start()

    barrier = pltpu.get_barrier_semaphore()
    partners = zpeer + [sib]
    for peer in line_peer:
        partners += [peer(k, cc) for k in (1, 2, 3) for cc in (c, 1 - c)]
    for k in (1, 2, 3):
        partners.append((w, (1 - yh) * 4 + wrap(x + k, 4)))
    for dev in partners:
        pl.semaphore_signal(barrier, inc=1, device_id=dev, device_id_type=MESH)

    sent = []

    def remote(src, dst, ss, rs, dev):
        return pltpu.make_async_remote_copy(
            src_ref=src, dst_ref=dst, send_sem=ss, recv_sem=rs, device_id=dev, device_id_type=MESH
        )

    def send(*a):
        cp = remote(*a)
        cp.start()
        sent.append(cp)

    def block(q_):
        return pl.ds(pl.multiple_of(q_ * ROWS, ROWS), ROWS)

    def normalise(raw, ring, cross):
        def body(i):
            rows = pl.ds(pl.multiple_of(i * 32, 32), 32)
            v = raw[rows, :].astype(F32)
            inv = 1.0 / jnp.sqrt(jnp.sum(v * v, -1, keepdims=True) + 1e-06)
            u = (v * inv).astype(BF16)
            ring[z, rows, :] = u
            cross[pl.ds(pl.multiple_of(q * ROWS + i * 32, 32), 32), :] = u

        loop(ROWS // 32, body)

    loads[0].wait()
    normalise(route_ref, ring_r, cross_r)
    t_own = jnp.concatenate(
        [target_ref[...].astype(F32), jnp.zeros((1, 256 - ROWS), F32)], axis=1
    )
    tring[z] = t_own
    tcross[q] = t_own

    pl.semaphore_wait(barrier, len(partners))

    rings = (ring_r, ring_m)

    def exists(d, k, h):
        return k < 3 or (k == 3 and h // 2 == d)

    def ring_copy(a, d, k, h, slot):
        i = ((a * 2 + d) * 4 + k) * 4 + h
        part = rings[a].at[slot, pl.ds(*PIECES[h])]
        dev = zpeer[0] if d == 0 else zpeer[6]
        return remote(part, part, ring_ss.at[i], ring_rs.at[i], dev)

    def ring_send(a, d, k, h):
        cp = ring_copy(a, d, k, h, wrap(z - k, 8) if d == 0 else wrap(z + k, 8))
        cp.start()
        sent.append(cp)

    def ring_wait(a, d, k, h):
        ring_copy(a, d, k, h, wrap(z - 1 - k, 8) if d == 0 else wrap(z + 1 + k, 8)).wait_recv()

    order_of = ((0, 1, 2, 3), (2, 3, 0, 1))

    def advance(a, k, places=(0, 1, 2, 3)):
        for o in places:
            for d in (0, 1):
                h = order_of[d][o]
                if exists(d, k, h):
                    ring_wait(a, d, k, h)
                    if exists(d, k + 1, h):
                        ring_send(a, d, k + 1, h)

    def ring_open(a):
        for o in range(4):
            for d in (0, 1):
                ring_send(a, d, 0, order_of[d][o])

    crosses = (cross_m, cross_r)
    b_own, b_sib = block(q), block(2 * y + 1 - c)
    b_across, b_diag = block(2 * (1 - y) + c), block(2 * (1 - y) + 1 - c)

    def cross_copy(a, i, blk, dev):
        part = crosses[a].at[blk]
        return remote(part, part, cross_ss.at[a * 3 + i], cross_rs.at[a * 3 + i], dev)

    def cross_send(a, i):
        cp = cross_copy(a, i, b_across if i == 2 else b_own, across if i == 0 else sib)
        cp.start()
        sent.append(cp)

    def cross_wait(a, i):
        cross_copy(a, i, (b_across, b_sib, b_diag)[i], sib).wait_recv()

    def target_ring():
        for k in range(1, 8):
            send(tring.at[z], tring.at[z], t_ss.at[k - 1], t_rs.at[k - 1], zpeer[k - 1])

    def target_ring_wait():
        for k in range(1, 8):
            at = tring.at[wrap(z - k, 8)]
            remote(at, at, t_ss.at[k - 1], t_rs.at[k - 1], sib).wait_recv()

    ring_open(0)
    loads[1].wait()
    normalise(mol_ref, ring_m, cross_m)
    cross_send(0, 0)
    for i, dev in enumerate((across, sib, diag)):
        send(tcross.at[q], tcross.at[q], t_ss.at[7 + i], t_rs.at[7 + i], dev)
    cross_send(0, 1)

    loads[2].wait()
    for t in range(16):
        tile = act_ref[:, 128 * t : 128 * t + 128].astype(F32)
        act_t[128 * t : 128 * t + 128, :] = tile.T

    def order(j):
        vv, xx = lax.div(j, 4), lax.rem(j, 4)
        yy, nn = lax.div(vv, 2), lax.rem(vv, 2) * 4 + xx
        for h in (0, 1):
            rows = [
                act_t[pl.ds(pl.multiple_of(1024 * yy + 128 * zz + 64 * h + 8 * nn, 8), 8), :]
                for zz in range(8)
            ]
            act_own[h, vv, xx] = jnp.concatenate(rows, axis=0).astype(BF16)

    loop(16, order)

    acts = (act_x, act_y)
    molds = (mold_x, mold_y)

    def act_part(l, h, at):
        return act_own.at[h, :, at] if l == 0 else act_own.at[h, at]

    own_acts = [
        pltpu.make_async_copy(act_part(l, c, line_at[l]), acts[l].at[line_at[l], c], in_s.at[3 + l])
        for l in (0, 1)
    ]
    for cp in own_acts:
        cp.start()

    def act_send(l):
        here = acts[l].at[line_at[l], c]
        for k in range(4):
            for o in (0, 1):
                if k + o > 0:
                    i = l * 8 + k * 2 + o
                    cc = c if o == 0 else 1 - c
                    src = act_part(l, cc, wrap(line_at[l] + k, 4))
                    send(src, here, act_ss.at[i], act_rs.at[i], line_peer[l](k, cc))

    def act_wait():
        for cp in own_acts:
            cp.wait()
        for l in (0, 1):
            for k in range(4):
                for o in (0, 1):
                    if k + o > 0:
                        i = l * 8 + k * 2 + o
                        cc = c if o == 0 else 1 - c
                        dst = acts[l].at[wrap(line_at[l] - k, 4), cc]
                        remote(dst, dst, act_ss.at[i], act_rs.at[i], sib).wait_recv()

    def mold_copy(l, k, o, j, p, cc, dev):
        i = ((l * 4 + k) * 2 + o) * 2 + j
        at = molds[l].at[p, cc, pl.ds(*CHUNKS[j])]
        return remote(at, at, mold_ss.at[i], mold_rs.at[i], dev)

    def mold_send(l, k, o, j):
        if o == 0:
            cp = mold_copy(l, k, o, j, line_at[l], c, line_peer[l](k, c))
        else:
            cp = mold_copy(l, k, o, j, wrap(line_at[l] - k, 4), c, sib)
        cp.start()
        sent.append(cp)

    def mold_wait(l, k, o, j):
        cc = c if o == 0 else 1 - c
        mold_copy(l, k, o, j, wrap(line_at[l] - k, 4), cc, sib).wait_recv()

    def mold_round(j):
        for k in (2, 1, 3):
            for l in (0, 1):
                mold_send(l, k, 0, j)
        for l in (0, 1):
            mold_send(l, 0, 1, j)

    def mold_pass(j):
        for k in (1, 3, 2):
            for l in (0, 1):
                mold_wait(l, k, 0, j)
                mold_send(l, k, 1, j)

    advance(0, 0)
    cross_wait(0, 0)
    cross_send(0, 2)

    for i, slot in enumerate((2 * (1 - y) + c, 2 * y + 1 - c, 2 * (1 - y) + 1 - c)):
        remote(
            tcross.at[slot], tcross.at[slot], t_ss.at[7 + i], t_rs.at[7 + i], sib
        ).wait_recv()
    eye = lax.broadcasted_iota(jnp.int32, (ROWS, ROWS), 0) == lax.broadcasted_iota(
        jnp.int32, (ROWS, ROWS), 1
    )
    for i in range(4):
        line = jnp.broadcast_to(tcross[i, 0:1, 0:ROWS], (ROWS, ROWS))
        col = jnp.sum(jnp.where(eye, line, 0.0), -1, keepdims=True)
        tcol[i * ROWS : (i + 1) * ROWS, :] = jnp.broadcast_to(col, (ROWS, 128))

    cross_wait(0, 1)
    cross_wait(0, 2)

    shift = shift_ref[0]
    seed = seed_ref[0]
    parts = (part_m, part_r)

    def pairs(a, slot, first=False):
        right = rings[a][slot]
        sharp = jnp.exp(jnp.full((1, ROWS), sharp_ref[0], F32))
        blocks = [pl.ds(i * ROWS, ROWS) for i in range(4)]

        def grads(i, s):
            if a == 0:
                ids = lax.broadcasted_iota(jnp.int32, (1, ROWS), 1) + wide_of(y, slot, c) * ROWS
                match = tcol[blocks[i], 0:1] == ids.astype(F32)
            else:
                base = wide_of(i // 2, z, i % 2) * ROWS
                ids = lax.broadcasted_iota(jnp.int32, (ROWS, 1), 0) + base
                match = ids.astype(F32) == tring[slot, 0:1, 0:ROWS]
            g = jax.nn.sigmoid(s * sharp + shift) - jnp.where(match, 1.0, 0.0)
            return (seed * g).astype(BF16)

        scores = [
            lax.dot_general(crosses[a][b, :], right, NT, preferred_element_type=F32)
            for b in blocks
        ]
        gs = [grads(i, s) for i, s in enumerate(scores)]
        for b, g in zip(blocks, gs):
            out = lax.dot_general(g, right, NN, preferred_element_type=F32)
            if first:
                parts[a][b, :] = out
            else:
                parts[a][b, :] += out

    def pairs_left(a, k):
        pairs(a, wrap(z - k, 8))

    def pairs_right(a, k):
        pairs(a, wrap(z + k, 8))

    def pairs_at(a, k):
        loop(2, lambda i: pairs(a, wrap(z + (2 * i - 1) * k, 8)))

    def reduce_copy(a, i, j):
        rows = pl.ds(*CHUNKS[j])
        dev = sib
        if i < 2:
            q_ = 2 * (1 - y) + 1 - c if i == 0 else 2 * y + 1 - c
            here = pl.ds(pl.multiple_of(q_ * ROWS + CHUNKS[j][0], 32), CHUNKS[j][1])
            src, dst = parts[a].at[here], sib_in.at[a, i, rows]
        elif i == 2:
            src, dst, dev = y_out.at[a, rows], y_in.at[a, rows], across
        else:
            src, dst, dev = a_out.at[a, j], a_in.at[a, j], across
        i = (a * 4 + i) * 2 + j
        return remote(src, dst, red_ss.at[i], red_rs.at[i], dev)

    def reduce_send(a, i, j):
        cp = reduce_copy(a, i, j)
        cp.start()
        sent.append(cp)

    def reduce_open(a):
        for i in (0, 1):
            for j in (0, 1):
                reduce_send(a, i, j)

    def diagonal(i):
        row = lax.broadcasted_iota(jnp.int32, (32, ROWS), 0) + i * 32
        return row == lax.broadcasted_iota(jnp.int32, (32, ROWS), 1)

    def blocks_of(j, body):
        first, size = CHUNKS[j]
        loop(size // 32, lambda i: body(i + first // 32))

    def reduce_across(a, j):
        a_out[a, j] = jnp.zeros((8, ROWS), F32)
        reduce_copy(a, 0, j).wait_recv()

        def body(i):
            rows = pl.ds(pl.multiple_of(i * 32, 32), 32)
            far = pl.ds(pl.multiple_of((2 * (1 - y) + c) * ROWS + i * 32, 32), 32)
            total = parts[a][far, :] + sib_in[a, 0, rows, :]
            unit = crosses[a][far, :].astype(F32)
            along = jnp.sum(total * unit, -1, keepdims=True)
            y_out[a, rows, :] = (total - along * unit).astype(BF16)
            spread = jnp.sum(jnp.where(diagonal(i), along, 0.0), 0, keepdims=True)
            a_out[a, j] += jnp.broadcast_to(spread, (8, ROWS))

        blocks_of(j, body)
        reduce_send(a, 2, j)
        reduce_send(a, 3, j)

    def reduce_close(a, j, raw, put):
        for i in (1, 2, 3):
            reduce_copy(a, i, j).wait_recv()

        def body(i):
            rows = pl.ds(pl.multiple_of(i * 32, 32), 32)
            own = pl.ds(pl.multiple_of(q * ROWS + i * 32, 32), 32)
            sharp = jnp.exp(jnp.full((32, 1), sharp_ref[0], F32))
            total = parts[a][own, :] + sib_in[a, 1, rows, :] + y_in[a, rows, :].astype(F32)
            along = jnp.sum(jnp.where(diagonal(i), a_in[a, j, 0:1, :], 0.0), -1, keepdims=True)
            total = total + along * crosses[a][own, :].astype(F32)
            v = raw[rows, :].astype(F32)
            inv = 1.0 / jnp.sqrt(jnp.sum(v * v, -1, keepdims=True) + 1e-06)
            unit = v * inv
            along = jnp.sum(unit * total, -1, keepdims=True)
            put(rows, ((total - unit * along) * (inv * sharp)).astype(BF16))

        blocks_of(j, body)

    def put_mold(rows, value):
        mold_x[x, c, rows, :] = value[:, : D // 2]
        mold_y[v, c, rows, :] = value[:, D // 2 :]

    def put_route(rows, value):
        route_out[rows, :] = value

    cross_send(1, 0)
    cross_send(1, 1)
    target_ring()
    act_send(0)
    act_send(1)
    pairs(0, z, True)
    pairs_left(0, 1)
    advance(0, 1, (0, 1))
    pairs_right(0, 1)
    advance(0, 1, (2, 3))
    pairs_left(0, 2)
    advance(0, 2, (0, 1))
    ring_open(1)
    pairs_right(0, 2)
    advance(0, 2, (2, 3))
    cross_wait(1, 0)
    cross_send(1, 2)
    pairs_at(0, 3)
    advance(0, 3)
    pairs_right(0, 4)

    reduce_open(0)
    cross_wait(1, 1)
    cross_wait(1, 2)
    target_ring_wait()
    reduce_across(0, 0)
    reduce_across(0, 1)
    advance(1, 0, (0, 1))
    pairs(1, z, True)
    advance(1, 0, (2, 3))
    pairs_left(1, 1)
    reduce_close(0, 0, mol_ref, put_mold)
    mold_round(0)
    advance(1, 1, (0, 1))
    reduce_close(0, 1, mol_ref, put_mold)
    mold_round(1)
    pairs_right(1, 1)
    advance(1, 1, (2, 3))
    mold_pass(0)
    pairs_left(1, 2)
    advance(1, 2, (0, 1))
    mold_pass(1)
    pairs_right(1, 2)
    act_wait()
    for j in (0, 1):
        for k in (0, 1, 3, 2):
            for l in (0, 1):
                mold_wait(l, k, 1, j)

    def weight(i):
        cols = pl.ds(pl.multiple_of(i * 256, 256), 256)
        for l in (0, 1):
            total = jnp.zeros((256, 256), F32)
            for p in range(4):
                for cc in (0, 1):
                    total += lax.dot_general(
                        acts[l][p, cc].reshape(256, ROWS),
                        molds[l][p, cc, :, cols],
                        NN,
                        preferred_element_type=F32,
                    )
            total = total.reshape(4, 64, 256)
            prod[l, :, :, cols] = total
            wsend[l, :, :, cols] = total.astype(BF16)

    loop(2, weight)
    for k in (2, 1, 3):
        for l in (0, 1):
            m = 1 - l
            i = l * 3 + k - 1
            src = wsend.at[l, wrap(line_at[m] + k, 4)]
            send(src, wrecv.at[l, line_at[m]], w_ss.at[i], w_rs.at[i], line_peer[m](k, c))

    advance(1, 2, (2, 3))
    pairs_at(1, 3)
    advance(1, 3)
    pairs_right(1, 4)
    reduce_open(1)
    reduce_across(1, 0)

    for l in (0, 1):
        for k in (1, 2, 3):
            i = l * 3 + k - 1
            at = wrecv.at[l, wrap(line_at[1 - l] - k, 4)]
            remote(at, at, w_ss.at[i], w_rs.at[i], sib).wait_recv()

    def gather_sum(i):
        rows = pl.ds(pl.multiple_of(i * 16, 16), 16)
        halves = []
        for l in (0, 1):
            total = prod[l, line_at[1 - l], rows, :]
            for k in (1, 2, 3):
                total += wrecv[l, wrap(line_at[1 - l] - k, 4), rows, :].astype(F32)
            halves.append(total)
        for o in (0, 1):
            both = jnp.concatenate([total[8 * o : 8 * o + 8, :] for total in halves], axis=0)
            zown[2 * i + o] = both
            zsend[2 * i + o] = both.astype(BF16)

    loop(4, gather_sum)
    for k in range(1, 8):
        src = zsend.at[wrap(z + k, 8)]
        send(src, zrecv.at[z], z_ss.at[k - 1], z_rs.at[k - 1], zpeer[k - 1])
    reduce_across(1, 1)
    total = zown[z]
    for k in range(1, 8):
        at = zrecv.at[wrap(z - k, 8)]
        remote(at, at, z_ss.at[k - 1], z_rs.at[k - 1], sib).wait_recv()
        total += zrecv[wrap(z - k, 8)].astype(F32)
    total = jnp.concatenate([total[0:8, :], total[8:16, :]], axis=1)
    gath[n] = total
    for k in (4, 2, 6, 1, 3, 5, 7):
        dev = (w, lax.rem(n + k, 8))
        send(gath.at[n], gath.at[n], g_ss.at[k - 1], g_rs.at[k - 1], dev)

    reduce_close(1, 0, route_ref, put_route)
    reduce_close(1, 1, route_ref, put_route)
    for k in range(1, 8):
        at = gath.at[lax.rem(n - k + 8, 8)]
        remote(at, at, g_ss.at[k - 1], g_rs.at[k - 1], sib).wait_recv()
    weight_out[...] = gath[...].reshape(64, D)
    for cp in sent:
        cp.wait_send()


def local(
    compound_activation,
    compound_vectors,
    pathway_vectors,
    matching_pathway_index,
    exponent_of_sharpness,
    offset_shift,
    objective_seed,
):
    vmem = pl.BlockSpec(memory_space=pltpu.VMEM)
    hbm = pl.BlockSpec(memory_space=pltpu.HBM)
    smem = pl.BlockSpec(memory_space=pltpu.SMEM)
    dma = pltpu.SemaphoreType.DMA
    weight_grad, route_grad = pl.pallas_call(
        kernel,
        out_shape=(
            pltpu.VMEM((64, D), F32),
            pltpu.VMEM((ROWS, D), BF16),
        ),
        in_specs=[hbm] * 3 + [vmem] + [smem] * 3,
        out_specs=(vmem, vmem),
        scratch_shapes=[
            pltpu.VMEM((ROWS, FF), BF16),
            pltpu.VMEM((ROWS, D), BF16),
            pltpu.VMEM((ROWS, D), BF16),
            pltpu.VMEM((8, ROWS, D), BF16),
            pltpu.VMEM((8, ROWS, D), BF16),
            pltpu.VMEM((4 * ROWS, D), BF16),
            pltpu.VMEM((4 * ROWS, D), BF16),
            pltpu.VMEM((8, 1, 256), F32),
            pltpu.VMEM((4, 1, 256), F32),
            pltpu.VMEM((4 * ROWS, 128), F32),
            pltpu.VMEM((4 * ROWS, D), F32),
            pltpu.VMEM((4 * ROWS, D), F32),
            pltpu.VMEM((2, 2, ROWS, D), F32),
            pltpu.VMEM((2, ROWS, D), BF16),
            pltpu.VMEM((2, ROWS, D), BF16),
            pltpu.VMEM((2, 2, 8, ROWS), F32),
            pltpu.VMEM((2, 2, 8, ROWS), F32),
            pltpu.VMEM((FF, ROWS), F32),
            pltpu.VMEM((2, 4, 4, 64, ROWS), BF16),
            pltpu.VMEM((4, 2, 4, 64, ROWS), BF16),
            pltpu.VMEM((4, 2, 4, 64, ROWS), BF16),
            pltpu.VMEM((4, 2, ROWS, D // 2), BF16),
            pltpu.VMEM((4, 2, ROWS, D // 2), BF16),
            pltpu.VMEM((2, 4, 64, D // 2), F32),
            pltpu.VMEM((2, 4, 64, D // 2), BF16),
            pltpu.VMEM((2, 4, 64, D // 2), BF16),
            pltpu.VMEM((8, 16, D // 2), F32),
            pltpu.VMEM((8, 16, D // 2), BF16),
            pltpu.VMEM((8, 16, D // 2), BF16),
            pltpu.VMEM((8, 8, D), F32),
            dma((64,)),
            dma((64,)),
            dma((6,)),
            dma((6,)),
            dma((10,)),
            dma((10,)),
            dma((16,)),
            dma((16,)),
            dma((5,)),
            dma((16,)),
            dma((16,)),
            dma((32,)),
            dma((32,)),
            dma((6,)),
            dma((6,)),
            dma((7,)),
            dma((7,)),
            dma((7,)),
            dma((7,)),
        ],
        compiler_params=pltpu.CompilerParams(
            collective_id=0, has_side_effects=True, vmem_limit_bytes=60 * 1024 * 1024
        ),
        name="contrastive_backward",
    )(
        compound_activation[0],
        compound_vectors[0],
        pathway_vectors[0],
        matching_pathway_index,
        exponent_of_sharpness,
        offset_shift,
        objective_seed,
    )
    return weight_grad, route_grad[None]


def solution(mesh):
    in_specs = (
        P("narrow", "wide", None),
        P("narrow", "wide", None),
        P("narrow", "wide", None),
        P("narrow", "wide"),
        P(),
        P(),
        P(),
    )
    out_specs = (P("wide", None), P("narrow", "wide", None))
    return jax.shard_map(local, mesh=mesh, in_specs=in_specs, out_specs=out_specs, check_vma=False)
```

```python
import jax
import jax.numpy as jnp
from jax import lax
from jax.experimental import pallas as pl
from jax.experimental.pallas import tpu as pltpu
from jax.sharding import PartitionSpec as P

ROWS = 160
PIECES = ((0, 48), (48, 32), (80, 48), (128, 32))
CHUNKS = ((0, 64), (64, 64), (128, 32))
D = 1024
FF = 2048
HALF = 80
F32 = jnp.float32
BF16 = jnp.bfloat16
MESH = pl.DeviceIdType.MESH
NT = (((1,), (1,)), ((), ()))
NN = (((1,), (0,)), ((), ()))
TN = (((0,), (0,)), ((), ()))


def wide_of(y, z, c):
    return y * 16 + z * 2 + c


def wrap(i, n):
    return lax.rem(i + n, n)


def loop(n, body):
    lax.fori_loop(0, n, lambda i, _: (body(i), 0)[1], 0)


def kernel(
    act_hbm,
    mol_hbm,
    route_hbm,
    target_ref,
    sharp_ref,
    shift_ref,
    seed_ref,
    weight_out,
    route_out,
    act_ref,
    mol_ref,
    route_ref,
    ring_r,
    cross_m,
    tcross,
    tcol,
    part_m,
    part_r,
    back_out,
    back_in,
    back_along,
    along_in,
    sib_in,
    y_out,
    y_in,
    a_out,
    a_in,
    act_t,
    act_own,
    act_x,
    act_y,
    mold_x,
    mold_y,
    prod,
    wsend,
    wrecv,
    zown,
    zsend,
    zrecv,
    gath,
    ring_ss,
    ring_rs,
    back_ss,
    back_rs,
    along_ss,
    along_rs,
    cross_ss,
    cross_rs,
    t_ss,
    t_rs,
    red_ss,
    red_rs,
    in_s,
    act_ss,
    act_rs,
    mold_ss,
    mold_rs,
    w_ss,
    w_rs,
    z_ss,
    z_rs,
    g_ss,
    g_rs,
):
    w = lax.axis_index("wide")
    n = lax.axis_index("narrow")
    y = lax.div(w, 16)
    z = lax.rem(lax.div(w, 2), 8)
    c = lax.rem(w, 2)
    q = 2 * y + c
    sib = (wide_of(y, z, 1 - c), n)
    across = (wide_of(1 - y, z, c), n)
    diag = (wide_of(1 - y, z, 1 - c), n)
    zpeer = [(wide_of(y, wrap(z + k, 8), c), n) for k in range(1, 8)]

    x = lax.rem(n, 4)
    yh = lax.div(n, 4)
    v = 2 * y + yh

    def x_peer(k, cc):
        return (wide_of(y, z, cc), yh * 4 + wrap(x + k, 4))

    def y_peer(k, cc):
        far = wrap(v + k, 4)
        return (wide_of(lax.div(far, 2), z, cc), lax.rem(far, 2) * 4 + x)

    line_peer = (x_peer, y_peer)
    line_at = (x, v)

    loads = [
        pltpu.make_async_copy(src, dst, in_s.at[i])
        for i, (src, dst) in enumerate(
            ((route_hbm, route_ref), (mol_hbm, mol_ref), (act_hbm, act_ref))
        )
    ]
    for cp in loads:
        cp.start()

    barrier = pltpu.get_barrier_semaphore()
    partners = zpeer + [sib]
    for peer in line_peer:
        partners += [peer(k, cc) for k in (1, 2, 3) for cc in (c, 1 - c)]
    for k in (1, 2, 3):
        partners.append((w, (1 - yh) * 4 + wrap(x + k, 4)))
    for dev in partners:
        pl.semaphore_signal(barrier, inc=1, device_id=dev, device_id_type=MESH)

    sent = []

    def remote(src, dst, ss, rs, dev):
        return pltpu.make_async_remote_copy(
            src_ref=src, dst_ref=dst, send_sem=ss, recv_sem=rs, device_id=dev, device_id_type=MESH
        )

    def send(*a):
        cp = remote(*a)
        cp.start()
        sent.append(cp)

    def block(q_):
        return pl.ds(pl.multiple_of(q_ * ROWS, ROWS), ROWS)

    def unit_rows(raw, rows):
        v = raw[rows, :].astype(F32)
        inv = 1.0 / jnp.sqrt(jnp.sum(v * v, -1, keepdims=True) + 1e-06)
        return v * inv, inv

    def normalise(raw, put):
        def body(i):
            rows = pl.ds(pl.multiple_of(i * 32, 32), 32)
            put(i, rows, unit_rows(raw, rows)[0].astype(BF16))

        loop(ROWS // 32, body)

    def put_ring(i, rows, u):
        ring_r[z, rows, :] = u

    def put_cross(i, rows, u):
        cross_m[pl.ds(pl.multiple_of(q * ROWS + i * 32, 32), 32), :] = u

    loads[0].wait()
    normalise(route_ref, put_ring)
    tcross[q] = jnp.concatenate(
        [target_ref[...].astype(F32), jnp.zeros((1, 256 - ROWS), F32)], axis=1
    )

    pl.semaphore_wait(barrier, len(partners))

    def exists(d, k, h):
        return k < 3 or (k == 3 and h // 2 == d)

    def ring_copy(d, k, h, slot):
        i = (d * 4 + k) * 4 + h
        part = ring_r.at[slot, pl.ds(*PIECES[h])]
        dev = zpeer[0] if d == 0 else zpeer[6]
        return remote(part, part, ring_ss.at[i], ring_rs.at[i], dev)

    def ring_send(d, k, h):
        cp = ring_copy(d, k, h, wrap(z - k, 8) if d == 0 else wrap(z + k, 8))
        cp.start()
        sent.append(cp)

    def ring_wait(d, k, h):
        ring_copy(d, k, h, wrap(z - 1 - k, 8) if d == 0 else wrap(z + 1 + k, 8)).wait_recv()

    order_of = ((0, 1, 2, 3), (2, 3, 0, 1))

    def advance(k, places=(0, 1, 2, 3)):
        for o in places:
            for d in (0, 1):
                h = order_of[d][o]
                if exists(d, k, h):
                    ring_wait(d, k, h)
                    if exists(d, k + 1, h):
                        ring_send(d, k + 1, h)

    def ring_open():
        for o in range(4):
            for d in (0, 1):
                ring_send(d, 0, order_of[d][o])

    b_own, b_sib = block(q), block(2 * y + 1 - c)
    b_across, b_diag = block(2 * (1 - y) + c), block(2 * (1 - y) + 1 - c)

    def cross_copy(i, blk, dev):
        part = cross_m.at[blk]
        return remote(part, part, cross_ss.at[i], cross_rs.at[i], dev)

    def cross_send(i):
        cp = cross_copy(i, b_across if i == 2 else b_own, across if i == 0 else sib)
        cp.start()
        sent.append(cp)

    def cross_wait(i):
        cross_copy(i, (b_across, b_sib, b_diag)[i], sib).wait_recv()

    ring_open()
    loads[1].wait()
    normalise(mol_ref, put_cross)
    cross_send(0)
    for i, dev in enumerate((across, sib, diag)):
        send(tcross.at[q], tcross.at[q], t_ss.at[i], t_rs.at[i], dev)
    cross_send(1)

    loads[2].wait()
    for t in range(16):
        tile = act_ref[:, 128 * t : 128 * t + 128].astype(F32)
        act_t[128 * t : 128 * t + 128, :] = tile.T

    def order(j):
        vv, xx = lax.div(j, 4), lax.rem(j, 4)
        yy, nn = lax.div(vv, 2), lax.rem(vv, 2) * 4 + xx
        for h in (0, 1):
            rows = [
                act_t[pl.ds(pl.multiple_of(1024 * yy + 128 * zz + 64 * h + 8 * nn, 8), 8), :]
                for zz in range(8)
            ]
            act_own[h, vv, xx] = jnp.concatenate(rows, axis=0).astype(BF16)

    loop(16, order)

    acts = (act_x, act_y)
    molds = (mold_x, mold_y)

    def act_part(l, h, at):
        return act_own.at[h, :, at] if l == 0 else act_own.at[h, at]

    own_acts = [
        pltpu.make_async_copy(act_part(l, c, line_at[l]), acts[l].at[line_at[l], c], in_s.at[3 + l])
        for l in (0, 1)
    ]
    for cp in own_acts:
        cp.start()

    def act_send(l):
        here = acts[l].at[line_at[l], c]
        for k in range(4):
            for o in (0, 1):
                if k + o > 0:
                    i = l * 8 + k * 2 + o
                    cc = c if o == 0 else 1 - c
                    src = act_part(l, cc, wrap(line_at[l] + k, 4))
                    send(src, here, act_ss.at[i], act_rs.at[i], line_peer[l](k, cc))

    def act_wait():
        for cp in own_acts:
            cp.wait()
        for l in (0, 1):
            for k in range(4):
                for o in (0, 1):
                    if k + o > 0:
                        i = l * 8 + k * 2 + o
                        cc = c if o == 0 else 1 - c
                        dst = acts[l].at[wrap(line_at[l] - k, 4), cc]
                        remote(dst, dst, act_ss.at[i], act_rs.at[i], sib).wait_recv()

    def mold_copy(l, k, o, j, p, cc, dev):
        i = ((l * 4 + k) * 2 + o) * 3 + j
        at = molds[l].at[p, cc, pl.ds(*CHUNKS[j])]
        return remote(at, at, mold_ss.at[i], mold_rs.at[i], dev)

    def mold_send(l, k, o, j):
        if o == 0:
            cp = mold_copy(l, k, o, j, line_at[l], c, line_peer[l](k, c))
        else:
            cp = mold_copy(l, k, o, j, wrap(line_at[l] - k, 4), c, sib)
        cp.start()
        sent.append(cp)

    def mold_wait(l, k, o, j):
        cc = c if o == 0 else 1 - c
        mold_copy(l, k, o, j, wrap(line_at[l] - k, 4), cc, sib).wait_recv()

    def mold_round(j):
        for k in (2, 1, 3):
            for l in (0, 1):
                mold_send(l, k, 0, j)
        for l in (0, 1):
            mold_send(l, 0, 1, j)

    def mold_pass(j):
        for k in (1, 3, 2):
            for l in (0, 1):
                mold_wait(l, k, 0, j)
                mold_send(l, k, 1, j)

    advance(0)
    cross_wait(0)
    cross_send(2)

    for i, slot in enumerate((2 * (1 - y) + c, 2 * y + 1 - c, 2 * (1 - y) + 1 - c)):
        remote(
            tcross.at[slot], tcross.at[slot], t_ss.at[i], t_rs.at[i], sib
        ).wait_recv()
    eye = lax.broadcasted_iota(jnp.int32, (ROWS, ROWS), 0) == lax.broadcasted_iota(
        jnp.int32, (ROWS, ROWS), 1
    )
    for i in range(4):
        line = jnp.broadcast_to(tcross[i, 0:1, 0:ROWS], (ROWS, ROWS))
        col = jnp.sum(jnp.where(eye, line, 0.0), -1, keepdims=True)
        tcol[i * ROWS : (i + 1) * ROWS, :] = jnp.broadcast_to(col, (ROWS, 128))

    cross_wait(1)
    cross_wait(2)

    shift = shift_ref[0]
    seed = seed_ref[0]

    def pairs(k, first=False):
        slot = wrap(z + k, 8)
        right = ring_r[slot]
        sharp = jnp.exp(jnp.full((1, ROWS), sharp_ref[0], F32))
        ids = lax.broadcasted_iota(jnp.int32, (1, ROWS), 1) + wide_of(y, slot, c) * ROWS
        ids = ids.astype(F32)
        blocks = [pl.ds(i * ROWS, ROWS) for i in range(4)]

        def grads(b, s):
            match = tcol[b, 0:1] == ids
            g = jax.nn.sigmoid(s * sharp + shift) - jnp.where(match, 1.0, 0.0)
            return (seed * g).astype(BF16)

        scores = [
            lax.dot_general(cross_m[b, :], right, NT, preferred_element_type=F32) for b in blocks
        ]
        gs = [grads(b, s) for b, s in zip(blocks, scores)]
        for b, g in zip(blocks, gs):
            out = lax.dot_general(g, right, NN, preferred_element_type=F32)
            if first:
                part_m[b, :] = out
            else:
                part_m[b, :] += out
        part_r[slot] = lax.dot_general(
            jnp.concatenate(gs, axis=0), cross_m[...], TN, preferred_element_type=F32
        )

    def back_copy(d, s, h):
        rows = pl.ds(h * HALF, HALF)
        i = (d * 4 + s) * 2 + h
        dev = zpeer[0] if d == 0 else zpeer[6]
        return remote(
            back_out.at[d, s, rows], back_in.at[d, s, rows], back_ss.at[i], back_rs.at[i], dev
        )

    def back_send(d, s, h):
        far = h == d
        k = 4 - s if d == 0 else 4 + s
        goal = wrap(z + k, 8)
        carried = s >= (1 if far else 2)
        if carried:
            back_copy(d, s - 1, h).wait_recv()
        spread = jnp.zeros((1, 256), F32)
        for first in range(h * HALF, h * HALF + HALF, 16):
            rows = pl.ds(first, 16)
            total = part_r[goal, rows, :]
            if carried:
                total += back_in[d, s - 1, rows, :].astype(F32)
            unit = ring_r[goal, rows, :].astype(F32)
            along = jnp.sum(total * unit, -1, keepdims=True)
            back_out[d, s, rows, :] = (total - along * unit).astype(BF16)
            place = lax.broadcasted_iota(jnp.int32, (16, 256), 0) + first
            place = place == lax.broadcasted_iota(jnp.int32, (16, 256), 1)
            spread += jnp.sum(jnp.where(place, along, 0.0), 0, keepdims=True)
        cp = back_copy(d, s, h)
        cp.start()
        sent.append(cp)
        if (d == 0) if s == 0 else not far:
            back_along[goal] = spread
        else:
            back_along[goal] += spread
            send(
                back_along.at[goal],
                along_in.at[z],
                along_ss.at[k - 1],
                along_rs.at[k - 1],
                zpeer[k - 1],
            )

    def back_near(s):
        back_send(0, s, 1)
        back_send(1, s, 0)

    def back_far(s):
        back_send(0, s, 0)
        back_send(1, s, 1)

    def back_close():
        for h in (1, 0):
            back_copy(0, 3, h).wait_recv()
            back_copy(1, 3, 1 - h).wait_recv()
        line = jnp.zeros((1, 256), F32)
        for k in range(1, 8):
            at = along_in.at[wrap(z - k, 8)]
            remote(at, at, along_ss.at[k - 1], along_rs.at[k - 1], sib).wait_recv()
            line += along_in[wrap(z - k, 8)]

        def body(i):
            rows = pl.ds(pl.multiple_of(i * 32, 32), 32)
            total = part_r[z, rows, :]
            for d in (0, 1):
                total += back_in[d, 3, rows, :].astype(F32)
            along = jnp.sum(jnp.where(diagonal(i), line[:, :ROWS], 0.0), -1, keepdims=True)
            total += along * ring_r[z, rows, :].astype(F32)
            route_out[rows, :] = norm_back(route_ref, rows, total)

        loop(ROWS // 32, body)

    def reduce_copy(i, j):
        rows = pl.ds(*CHUNKS[j])
        dev = sib
        if i < 2:
            q_ = 2 * (1 - y) + 1 - c if i == 0 else 2 * y + 1 - c
            here = pl.ds(pl.multiple_of(q_ * ROWS + CHUNKS[j][0], 32), CHUNKS[j][1])
            src, dst = part_m.at[here], sib_in.at[i, rows]
        elif i == 2:
            src, dst, dev = y_out.at[rows], y_in.at[rows], across
        else:
            src, dst, dev = a_out.at[j], a_in.at[j], across
        i = i * 3 + j
        return remote(src, dst, red_ss.at[i], red_rs.at[i], dev)

    def reduce_send(i, j):
        cp = reduce_copy(i, j)
        cp.start()
        sent.append(cp)

    def reduce_open():
        for i in (0, 1):
            for j in (0, 1, 2):
                reduce_send(i, j)

    def diagonal(i):
        row = lax.broadcasted_iota(jnp.int32, (32, ROWS), 0) + i * 32
        return row == lax.broadcasted_iota(jnp.int32, (32, ROWS), 1)

    def norm_back(raw, rows, total):
        unit, inv = unit_rows(raw, rows)
        sharp = jnp.exp(jnp.full((32, 1), sharp_ref[0], F32))
        along = jnp.sum(unit * total, -1, keepdims=True)
        return ((total - unit * along) * (inv * sharp)).astype(BF16)

    def blocks_of(j, body):
        first, size = CHUNKS[j]
        loop(size // 32, lambda i: body(i + first // 32))

    def reduce_across(j):
        a_out[j] = jnp.zeros((8, ROWS), F32)
        reduce_copy(0, j).wait_recv()

        def body(i):
            rows = pl.ds(pl.multiple_of(i * 32, 32), 32)
            far = pl.ds(pl.multiple_of((2 * (1 - y) + c) * ROWS + i * 32, 32), 32)
            total = part_m[far, :] + sib_in[0, rows, :]
            unit = cross_m[far, :].astype(F32)
            along = jnp.sum(total * unit, -1, keepdims=True)
            y_out[rows, :] = (total - along * unit).astype(BF16)
            spread = jnp.sum(jnp.where(diagonal(i), along, 0.0), 0, keepdims=True)
            a_out[j] += jnp.broadcast_to(spread, (8, ROWS))

        blocks_of(j, body)
        reduce_send(2, j)
        reduce_send(3, j)

    def reduce_close(j):
        for i in (1, 2, 3):
            reduce_copy(i, j).wait_recv()

        def body(i):
            rows = pl.ds(pl.multiple_of(i * 32, 32), 32)
            own = pl.ds(pl.multiple_of(q * ROWS + i * 32, 32), 32)
            total = part_m[own, :] + sib_in[1, rows, :] + y_in[rows, :].astype(F32)
            along = jnp.sum(jnp.where(diagonal(i), a_in[j, 0:1, :], 0.0), -1, keepdims=True)
            total = total + along * cross_m[own, :].astype(F32)
            value = norm_back(mol_ref, rows, total)
            mold_x[x, c, rows, :] = value[:, : D // 2]
            mold_y[v, c, rows, :] = value[:, D // 2 :]

        blocks_of(j, body)
        mold_round(j)

    act_send(0)
    act_send(1)
    pairs(0, True)
    pairs(-1)
    advance(1, (0, 1))
    pairs(1)
    advance(1, (2, 3))
    pairs(-2)
    advance(2, (0, 1))
    pairs(2)
    advance(2, (2, 3))
    pairs(-3)
    pairs(3)
    back_near(1)
    advance(3)
    pairs(4)

    reduce_open()
    back_far(0)
    reduce_across(0)
    reduce_across(1)
    reduce_across(2)
    back_near(2)
    reduce_close(0)
    back_far(1)
    reduce_close(1)
    reduce_close(2)
    back_near(3)
    mold_pass(0)
    back_far(2)
    mold_pass(1)
    mold_pass(2)
    act_wait()
    back_far(3)
    for j in (0, 1, 2):
        for k in (0, 1, 3, 2):
            for l in (0, 1):
                mold_wait(l, k, 1, j)

    def weight(l, half):
        total = jnp.zeros((256, 256), F32)
        for p in range(4):
            for cc in (0, 1):
                total += lax.dot_general(
                    acts[l][p, cc].reshape(256, ROWS),
                    molds[l][p, cc, :, 256 * half : 256 * half + 256],
                    NN,
                    preferred_element_type=F32,
                )
        total = total.reshape(4, 64, 256)
        prod[l, half] = total
        wsend[l, half] = total.astype(BF16)

    def weight_copy(l, half, k, src, slot):
        i = (l * 2 + half) * 3 + k - 1
        dst = wrecv.at[l, half, slot]
        return remote(src, dst, w_ss.at[i], w_rs.at[i], line_peer[1 - l](k, c))

    for half in (0, 1):
        for l in (0, 1):
            weight(l, half)
            here = line_at[1 - l]
            for k in (2, 1, 3):
                src = wsend.at[l, half, wrap(here + k, 4)]
                cp = weight_copy(l, half, k, src, here)
                cp.start()
                sent.append(cp)

    for half in (0, 1):
        for l in (0, 1):
            for k in (1, 3, 2):
                slot = wrap(line_at[1 - l] - k, 4)
                weight_copy(l, half, k, wrecv.at[l, half, slot], slot).wait_recv()

    def gather_sum(i):
        rows = pl.ds(pl.multiple_of(i * 16, 16), 16)
        for half in (0, 1):
            cols = slice(256 * half, 256 * half + 256)
            lines = []
            for l in (0, 1):
                total = prod[l, half, line_at[1 - l], rows, :]
                for k in (1, 2, 3):
                    total += wrecv[l, half, wrap(line_at[1 - l] - k, 4), rows, :].astype(F32)
                lines.append(total)
            for o in (0, 1):
                both = jnp.concatenate([total[8 * o : 8 * o + 8, :] for total in lines], axis=0)
                zown[2 * i + o, :, cols] = both
                zsend[2 * i + o, :, cols] = both.astype(BF16)

    loop(4, gather_sum)
    for k in range(1, 8):
        src = zsend.at[wrap(z + k, 8)]
        send(src, zrecv.at[z], z_ss.at[k - 1], z_rs.at[k - 1], zpeer[k - 1])
    back_close()
    total = zown[z]
    for k in range(1, 8):
        at = zrecv.at[wrap(z - k, 8)]
        remote(at, at, z_ss.at[k - 1], z_rs.at[k - 1], sib).wait_recv()
        total += zrecv[wrap(z - k, 8)].astype(F32)
    gath[n] = total.astype(BF16)
    for k in (4, 2, 6, 1, 3, 5, 7):
        dev = (w, lax.rem(n + k, 8))
        send(gath.at[n], gath.at[n], g_ss.at[k - 1], g_rs.at[k - 1], dev)

    for k in range(1, 8):
        at = gath.at[lax.rem(n - k + 8, 8)]
        remote(at, at, g_ss.at[k - 1], g_rs.at[k - 1], sib).wait_recv()
    for i in range(8):
        total = gath[i].astype(F32)
        weight_out[8 * i : 8 * i + 8, : D // 2] = total[0:8, :]
        weight_out[8 * i : 8 * i + 8, D // 2 :] = total[8:16, :]
    for cp in sent:
        cp.wait_send()


def local(
    compound_activation,
    compound_vectors,
    pathway_vectors,
    matching_pathway_index,
    exponent_of_sharpness,
    offset_shift,
    objective_seed,
):
    vmem = pl.BlockSpec(memory_space=pltpu.VMEM)
    hbm = pl.BlockSpec(memory_space=pltpu.HBM)
    smem = pl.BlockSpec(memory_space=pltpu.SMEM)
    dma = pltpu.SemaphoreType.DMA
    weight_grad, route_grad = pl.pallas_call(
        kernel,
        out_shape=(
            pltpu.VMEM((64, D), F32),
            pltpu.VMEM((ROWS, D), BF16),
        ),
        in_specs=[hbm] * 3 + [vmem] + [smem] * 3,
        out_specs=(vmem, vmem),
        scratch_shapes=[
            pltpu.VMEM((ROWS, FF), BF16),
            pltpu.VMEM((ROWS, D), BF16),
            pltpu.VMEM((ROWS, D), BF16),
            pltpu.VMEM((8, ROWS, D), BF16),
            pltpu.VMEM((4 * ROWS, D), BF16),
            pltpu.VMEM((4, 1, 256), F32),
            pltpu.VMEM((4 * ROWS, 128), F32),
            pltpu.VMEM((4 * ROWS, D), F32),
            pltpu.VMEM((8, ROWS, D), F32),
            pltpu.VMEM((2, 4, ROWS, D), BF16),
            pltpu.VMEM((2, 4, ROWS, D), BF16),
            pltpu.VMEM((8, 1, 256), F32),
            pltpu.VMEM((8, 1, 256), F32),
            pltpu.VMEM((2, ROWS, D), F32),
            pltpu.VMEM((ROWS, D), BF16),
            pltpu.VMEM((ROWS, D), BF16),
            pltpu.VMEM((3, 8, ROWS), F32),
            pltpu.VMEM((3, 8, ROWS), F32),
            pltpu.VMEM((FF, ROWS), F32),
            pltpu.VMEM((2, 4, 4, 64, ROWS), BF16),
            pltpu.VMEM((4, 2, 4, 64, ROWS), BF16),
            pltpu.VMEM((4, 2, 4, 64, ROWS), BF16),
            pltpu.VMEM((4, 2, ROWS, D // 2), BF16),
            pltpu.VMEM((4, 2, ROWS, D // 2), BF16),
            pltpu.VMEM((2, 2, 4, 64, D // 4), F32),
            pltpu.VMEM((2, 2, 4, 64, D // 4), BF16),
            pltpu.VMEM((2, 2, 4, 64, D // 4), BF16),
            pltpu.VMEM((8, 16, D // 2), F32),
            pltpu.VMEM((8, 16, D // 2), BF16),
            pltpu.VMEM((8, 16, D // 2), BF16),
            pltpu.VMEM((8, 16, D // 2), BF16),
            dma((32,)),
            dma((32,)),
            dma((16,)),
            dma((16,)),
            dma((7,)),
            dma((7,)),
            dma((3,)),
            dma((3,)),
            dma((3,)),
            dma((3,)),
            dma((12,)),
            dma((12,)),
            dma((5,)),
            dma((16,)),
            dma((16,)),
            dma((48,)),
            dma((48,)),
            dma((12,)),
            dma((12,)),
            dma((7,)),
            dma((7,)),
            dma((7,)),
            dma((7,)),
        ],
        compiler_params=pltpu.CompilerParams(
            collective_id=0, has_side_effects=True, vmem_limit_bytes=60 * 1024 * 1024
        ),
        name="contrastive_backward",
    )(
        compound_activation[0],
        compound_vectors[0],
        pathway_vectors[0],
        matching_pathway_index,
        exponent_of_sharpness,
        offset_shift,
        objective_seed,
    )
    return weight_grad, route_grad[None]


def solution(mesh):
    in_specs = (
        P("narrow", "wide", None),
        P("narrow", "wide", None),
        P("narrow", "wide", None),
        P("narrow", "wide"),
        P(),
        P(),
        P(),
    )
    out_specs = (P("wide", None), P("narrow", "wide", None))
    return jax.shard_map(local, mesh=mesh, in_specs=in_specs, out_specs=out_specs, check_vma=False)
```

```python
import jax
import jax.numpy as jnp
from jax import lax
from jax.experimental import pallas as pl
from jax.experimental.pallas import tpu as pltpu
from jax.sharding import PartitionSpec as P

ROWS = 160
PIECES = ((0, 48), (48, 32), (80, 48), (128, 32))
CHUNKS = ((0, 64), (64, 64), (128, 32))
D = 1024
FF = 2048
HALF = 80
F32 = jnp.float32
BF16 = jnp.bfloat16
MESH = pl.DeviceIdType.MESH
NT = (((1,), (1,)), ((), ()))
NN = (((1,), (0,)), ((), ()))
TN = (((0,), (0,)), ((), ()))


def wide_of(y, z, c):
    return y * 16 + z * 2 + c


def wrap(i, n):
    return lax.rem(i + n, n)


def loop(n, body):
    lax.fori_loop(0, n, lambda i, _: (body(i), 0)[1], 0)


def kernel(
    act_hbm,
    mol_hbm,
    route_hbm,
    target_ref,
    sharp_ref,
    shift_ref,
    seed_ref,
    weight_out,
    route_out,
    act_ref,
    mol_ref,
    route_ref,
    ring_r,
    cross_m,
    tcross,
    tcol,
    part_m,
    part_r,
    back_out,
    back_in,
    back_along,
    along_in,
    sib_in,
    y_out,
    y_in,
    a_out,
    a_in,
    act_t,
    act_own,
    act_x,
    act_y,
    mold_x,
    mold_y,
    prod,
    wsend,
    wrecv,
    zown,
    zsend,
    zrecv,
    gath,
    ring_ss,
    ring_rs,
    back_ss,
    back_rs,
    along_ss,
    along_rs,
    cross_ss,
    cross_rs,
    t_ss,
    t_rs,
    red_ss,
    red_rs,
    in_s,
    act_ss,
    act_rs,
    mold_ss,
    mold_rs,
    w_ss,
    w_rs,
    z_ss,
    z_rs,
    g_ss,
    g_rs,
):
    w = lax.axis_index("wide")
    n = lax.axis_index("narrow")
    y = lax.div(w, 16)
    z = lax.rem(lax.div(w, 2), 8)
    c = lax.rem(w, 2)
    q = 2 * y + c
    sib = (wide_of(y, z, 1 - c), n)
    across = (wide_of(1 - y, z, c), n)
    diag = (wide_of(1 - y, z, 1 - c), n)
    zpeer = [(wide_of(y, wrap(z + k, 8), c), n) for k in range(1, 8)]

    x = lax.rem(n, 4)
    yh = lax.div(n, 4)
    v = 2 * y + yh

    def x_peer(k, cc):
        return (wide_of(y, z, cc), yh * 4 + wrap(x + k, 4))

    def y_peer(k, cc):
        far = wrap(v + k, 4)
        return (wide_of(lax.div(far, 2), z, cc), lax.rem(far, 2) * 4 + x)

    line_peer = (x_peer, y_peer)
    line_at = (x, v)

    loads = [
        pltpu.make_async_copy(src, dst, in_s.at[i])
        for i, (src, dst) in enumerate(
            ((route_hbm, route_ref), (mol_hbm, mol_ref), (act_hbm, act_ref))
        )
    ]
    for cp in loads:
        cp.start()

    barrier = pltpu.get_barrier_semaphore()
    partners = zpeer + [sib]
    for peer in line_peer:
        partners += [peer(k, cc) for k in (1, 2, 3) for cc in (c, 1 - c)]
    for k in (1, 2, 3):
        partners.append((w, (1 - yh) * 4 + wrap(x + k, 4)))
    for dev in partners:
        pl.semaphore_signal(barrier, inc=1, device_id=dev, device_id_type=MESH)

    sent = []

    def remote(src, dst, ss, rs, dev):
        return pltpu.make_async_remote_copy(
            src_ref=src, dst_ref=dst, send_sem=ss, recv_sem=rs, device_id=dev, device_id_type=MESH
        )

    def send(*a):
        cp = remote(*a)
        cp.start()
        sent.append(cp)

    def block(q_):
        return pl.ds(pl.multiple_of(q_ * ROWS, ROWS), ROWS)

    def unit_rows(raw, rows):
        v = raw[rows, :].astype(F32)
        inv = 1.0 / jnp.sqrt(jnp.sum(v * v, -1, keepdims=True) + 1e-06)
        return v * inv, inv

    def normalise(raw, put):
        def body(i):
            rows = pl.ds(pl.multiple_of(i * 32, 32), 32)
            put(i, rows, unit_rows(raw, rows)[0].astype(BF16))

        loop(ROWS // 32, body)

    def put_ring(i, rows, u):
        ring_r[z, rows, :] = u

    def put_cross(i, rows, u):
        cross_m[pl.ds(pl.multiple_of(q * ROWS + i * 32, 32), 32), :] = u

    loads[0].wait()
    normalise(route_ref, put_ring)
    tcross[q] = jnp.concatenate(
        [target_ref[...].astype(F32), jnp.zeros((1, 256 - ROWS), F32)], axis=1
    )

    pl.semaphore_wait(barrier, len(partners))

    def exists(d, k, h):
        return k < 3 or (k == 3 and h // 2 == d)

    def ring_copy(d, k, h, slot):
        i = (d * 4 + k) * 4 + h
        part = ring_r.at[slot, pl.ds(*PIECES[h])]
        dev = zpeer[0] if d == 0 else zpeer[6]
        return remote(part, part, ring_ss.at[i], ring_rs.at[i], dev)

    def ring_send(d, k, h):
        cp = ring_copy(d, k, h, wrap(z - k, 8) if d == 0 else wrap(z + k, 8))
        cp.start()
        sent.append(cp)

    def ring_wait(d, k, h):
        ring_copy(d, k, h, wrap(z - 1 - k, 8) if d == 0 else wrap(z + 1 + k, 8)).wait_recv()

    order_of = ((0, 1, 2, 3), (2, 3, 0, 1))

    def advance(k, places=(0, 1, 2, 3)):
        for o in places:
            for d in (0, 1):
                h = order_of[d][o]
                if exists(d, k, h):
                    ring_wait(d, k, h)
                    if exists(d, k + 1, h):
                        ring_send(d, k + 1, h)

    def ring_open():
        for o in range(4):
            for d in (0, 1):
                ring_send(d, 0, order_of[d][o])

    b_own, b_sib = block(q), block(2 * y + 1 - c)
    b_across, b_diag = block(2 * (1 - y) + c), block(2 * (1 - y) + 1 - c)

    def cross_copy(i, blk, dev):
        part = cross_m.at[blk]
        return remote(part, part, cross_ss.at[i], cross_rs.at[i], dev)

    def cross_send(i):
        cp = cross_copy(i, b_across if i == 2 else b_own, across if i == 0 else sib)
        cp.start()
        sent.append(cp)

    def cross_wait(i):
        cross_copy(i, (b_across, b_sib, b_diag)[i], sib).wait_recv()

    ring_open()
    loads[1].wait()
    normalise(mol_ref, put_cross)
    cross_send(0)
    for i, dev in enumerate((across, sib, diag)):
        send(tcross.at[q], tcross.at[q], t_ss.at[i], t_rs.at[i], dev)
    cross_send(1)

    loads[2].wait()
    for t in range(16):
        tile = act_ref[:, 128 * t : 128 * t + 128].astype(F32)
        act_t[128 * t : 128 * t + 128, :] = tile.T

    def order(j):
        vv, xx = lax.div(j, 4), lax.rem(j, 4)
        yy, nn = lax.div(vv, 2), lax.rem(vv, 2) * 4 + xx
        for h in (0, 1):
            rows = [
                act_t[pl.ds(pl.multiple_of(1024 * yy + 128 * zz + 64 * h + 8 * nn, 8), 8), :]
                for zz in range(8)
            ]
            act_own[h, vv, xx] = jnp.concatenate(rows, axis=0).astype(BF16)

    loop(16, order)

    acts = (act_x, act_y)
    molds = (mold_x, mold_y)

    def act_part(l, h, at):
        return act_own.at[h, :, at] if l == 0 else act_own.at[h, at]

    own_acts = [
        pltpu.make_async_copy(act_part(l, c, line_at[l]), acts[l].at[line_at[l], c], in_s.at[3 + l])
        for l in (0, 1)
    ]
    for cp in own_acts:
        cp.start()

    def act_send(l):
        here = acts[l].at[line_at[l], c]
        for k in range(4):
            for o in (0, 1):
                if k + o > 0:
                    i = l * 8 + k * 2 + o
                    cc = c if o == 0 else 1 - c
                    src = act_part(l, cc, wrap(line_at[l] + k, 4))
                    send(src, here, act_ss.at[i], act_rs.at[i], line_peer[l](k, cc))

    def act_wait():
        for cp in own_acts:
            cp.wait()
        for l in (0, 1):
            for k in range(4):
                for o in (0, 1):
                    if k + o > 0:
                        i = l * 8 + k * 2 + o
                        cc = c if o == 0 else 1 - c
                        dst = acts[l].at[wrap(line_at[l] - k, 4), cc]
                        remote(dst, dst, act_ss.at[i], act_rs.at[i], sib).wait_recv()

    def mold_copy(l, k, o, j, p, cc, dev):
        i = ((l * 4 + k) * 2 + o) * 3 + j
        at = molds[l].at[p, cc, pl.ds(*CHUNKS[j])]
        return remote(at, at, mold_ss.at[i], mold_rs.at[i], dev)

    def mold_send(l, k, o, j):
        if o == 0:
            cp = mold_copy(l, k, o, j, line_at[l], c, line_peer[l](k, c))
        else:
            cp = mold_copy(l, k, o, j, wrap(line_at[l] - k, 4), c, sib)
        cp.start()
        sent.append(cp)

    def mold_wait(l, k, o, j):
        cc = c if o == 0 else 1 - c
        mold_copy(l, k, o, j, wrap(line_at[l] - k, 4), cc, sib).wait_recv()

    def mold_round(j):
        for k in (2, 1, 3):
            for l in (0, 1):
                mold_send(l, k, 0, j)
        for l in (0, 1):
            mold_send(l, 0, 1, j)

    def mold_pass(j):
        for k in (1, 3, 2):
            for l in (0, 1):
                mold_wait(l, k, 0, j)
                mold_send(l, k, 1, j)

    advance(0)
    cross_wait(0)
    cross_send(2)

    for i, slot in enumerate((2 * (1 - y) + c, 2 * y + 1 - c, 2 * (1 - y) + 1 - c)):
        remote(
            tcross.at[slot], tcross.at[slot], t_ss.at[i], t_rs.at[i], sib
        ).wait_recv()
    eye = lax.broadcasted_iota(jnp.int32, (ROWS, ROWS), 0) == lax.broadcasted_iota(
        jnp.int32, (ROWS, ROWS), 1
    )
    for i in range(4):
        line = jnp.broadcast_to(tcross[i, 0:1, 0:ROWS], (ROWS, ROWS))
        col = jnp.sum(jnp.where(eye, line, 0.0), -1, keepdims=True)
        tcol[i * ROWS : (i + 1) * ROWS, :] = jnp.broadcast_to(col, (ROWS, 128))

    cross_wait(1)
    cross_wait(2)

    shift = shift_ref[0]
    seed = seed_ref[0]

    def pairs(k, first=False):
        slot = wrap(z + k, 8)
        right = ring_r[slot]
        sharp = jnp.exp(jnp.full((1, ROWS), sharp_ref[0], F32))
        ids = lax.broadcasted_iota(jnp.int32, (1, ROWS), 1) + wide_of(y, slot, c) * ROWS
        ids = ids.astype(F32)
        blocks = [pl.ds(i * ROWS, ROWS) for i in range(4)]

        def grads(b, s):
            match = tcol[b, 0:1] == ids
            g = jax.nn.sigmoid(s * sharp + shift) - jnp.where(match, 1.0, 0.0)
            return (seed * g).astype(BF16)

        scores = [
            lax.dot_general(cross_m[b, :], right, NT, preferred_element_type=F32) for b in blocks
        ]
        gs = [grads(b, s) for b, s in zip(blocks, scores)]
        for b, g in zip(blocks, gs):
            out = lax.dot_general(g, right, NN, preferred_element_type=F32)
            if first:
                part_m[b, :] = out
            else:
                part_m[b, :] += out
        part_r[slot] = lax.dot_general(
            jnp.concatenate(gs, axis=0), cross_m[...], TN, preferred_element_type=F32
        )

    def back_copy(d, s, h):
        rows = pl.ds(h * HALF, HALF)
        i = (d * 4 + s) * 2 + h
        dev = zpeer[0] if d == 0 else zpeer[6]
        return remote(
            back_out.at[d, s, rows], back_in.at[d, s, rows], back_ss.at[i], back_rs.at[i], dev
        )

    def back_send(d, s, h):
        far = h == d
        k = 4 - s if d == 0 else 4 + s
        goal = wrap(z + k, 8)
        carried = s >= (1 if far else 2)
        if carried:
            back_copy(d, s - 1, h).wait_recv()
        spread = jnp.zeros((1, 256), F32)
        for first in range(h * HALF, h * HALF + HALF, 16):
            rows = pl.ds(first, 16)
            total = part_r[goal, rows, :]
            if carried:
                total += back_in[d, s - 1, rows, :].astype(F32)
            unit = ring_r[goal, rows, :].astype(F32)
            along = jnp.sum(total * unit, -1, keepdims=True)
            back_out[d, s, rows, :] = (total - along * unit).astype(BF16)
            place = lax.broadcasted_iota(jnp.int32, (16, 256), 0) + first
            place = place == lax.broadcasted_iota(jnp.int32, (16, 256), 1)
            spread += jnp.sum(jnp.where(place, along, 0.0), 0, keepdims=True)
        cp = back_copy(d, s, h)
        cp.start()
        sent.append(cp)
        if (d == 0) if s == 0 else not far:
            back_along[goal] = spread
        else:
            back_along[goal] += spread
            send(
                back_along.at[goal],
                along_in.at[z],
                along_ss.at[k - 1],
                along_rs.at[k - 1],
                zpeer[k - 1],
            )

    def back_near(s):
        back_send(0, s, 1)
        back_send(1, s, 0)

    def back_far(s):
        back_send(0, s, 0)
        back_send(1, s, 1)

    def back_close():
        for h in (1, 0):
            back_copy(0, 3, h).wait_recv()
            back_copy(1, 3, 1 - h).wait_recv()
        line = jnp.zeros((1, 256), F32)
        for k in range(1, 8):
            at = along_in.at[wrap(z - k, 8)]
            remote(at, at, along_ss.at[k - 1], along_rs.at[k - 1], sib).wait_recv()
            line += along_in[wrap(z - k, 8)]

        def body(i):
            rows = pl.ds(pl.multiple_of(i * 32, 32), 32)
            total = part_r[z, rows, :]
            for d in (0, 1):
                total += back_in[d, 3, rows, :].astype(F32)
            along = jnp.sum(jnp.where(diagonal(i), line[:, :ROWS], 0.0), -1, keepdims=True)
            total += along * ring_r[z, rows, :].astype(F32)
            route_out[rows, :] = norm_back(route_ref, rows, total)

        loop(ROWS // 32, body)

    def reduce_copy(i, j):
        rows = pl.ds(*CHUNKS[j])
        dev = sib
        if i < 2:
            q_ = 2 * (1 - y) + 1 - c if i == 0 else 2 * y + 1 - c
            here = pl.ds(pl.multiple_of(q_ * ROWS + CHUNKS[j][0], 32), CHUNKS[j][1])
            src, dst = part_m.at[here], sib_in.at[i, rows]
        elif i == 2:
            src, dst, dev = y_out.at[rows], y_in.at[rows], across
        else:
            src, dst, dev = a_out.at[j], a_in.at[j], across
        i = i * 3 + j
        return remote(src, dst, red_ss.at[i], red_rs.at[i], dev)

    def reduce_send(i, j):
        cp = reduce_copy(i, j)
        cp.start()
        sent.append(cp)

    def reduce_open():
        for i in (0, 1):
            for j in (0, 1, 2):
                reduce_send(i, j)

    def diagonal(i):
        row = lax.broadcasted_iota(jnp.int32, (32, ROWS), 0) + i * 32
        return row == lax.broadcasted_iota(jnp.int32, (32, ROWS), 1)

    def norm_back(raw, rows, total):
        unit, inv = unit_rows(raw, rows)
        sharp = jnp.exp(jnp.full((32, 1), sharp_ref[0], F32))
        along = jnp.sum(unit * total, -1, keepdims=True)
        return ((total - unit * along) * (inv * sharp)).astype(BF16)

    def blocks_of(j, body):
        first, size = CHUNKS[j]
        loop(size // 32, lambda i: body(i + first // 32))

    def reduce_across(j):
        a_out[j] = jnp.zeros((8, ROWS), F32)
        reduce_copy(0, j).wait_recv()

        def body(i):
            rows = pl.ds(pl.multiple_of(i * 32, 32), 32)
            far = pl.ds(pl.multiple_of((2 * (1 - y) + c) * ROWS + i * 32, 32), 32)
            total = part_m[far, :] + sib_in[0, rows, :]
            unit = cross_m[far, :].astype(F32)
            along = jnp.sum(total * unit, -1, keepdims=True)
            y_out[rows, :] = (total - along * unit).astype(BF16)
            spread = jnp.sum(jnp.where(diagonal(i), along, 0.0), 0, keepdims=True)
            a_out[j] += jnp.broadcast_to(spread, (8, ROWS))

        blocks_of(j, body)
        reduce_send(2, j)
        reduce_send(3, j)

    def reduce_close(j):
        for i in (1, 2, 3):
            reduce_copy(i, j).wait_recv()

        def body(i):
            rows = pl.ds(pl.multiple_of(i * 32, 32), 32)
            own = pl.ds(pl.multiple_of(q * ROWS + i * 32, 32), 32)
            total = part_m[own, :] + sib_in[1, rows, :] + y_in[rows, :].astype(F32)
            along = jnp.sum(jnp.where(diagonal(i), a_in[j, 0:1, :], 0.0), -1, keepdims=True)
            total = total + along * cross_m[own, :].astype(F32)
            value = norm_back(mol_ref, rows, total)
            mold_x[x, c, rows, :] = value[:, : D // 2]
            mold_y[v, c, rows, :] = value[:, D // 2 :]

        blocks_of(j, body)
        mold_round(j)

    act_send(0)
    act_send(1)
    pairs(0, True)
    pairs(-1)
    advance(1, (0, 1))
    pairs(1)
    advance(1, (2, 3))
    pairs(-2)
    advance(2, (0, 1))
    pairs(2)
    advance(2, (2, 3))
    pairs(-3)
    pairs(3)
    back_near(1)
    advance(3)
    pairs(4)

    reduce_open()
    back_far(0)
    reduce_across(0)
    reduce_across(1)
    reduce_across(2)
    back_near(2)
    reduce_close(0)
    back_far(1)
    reduce_close(1)
    reduce_close(2)
    back_near(3)
    mold_pass(0)
    back_far(2)
    mold_pass(1)
    mold_pass(2)
    act_wait()
    for j in (0, 1, 2):
        for k in (0, 1, 3, 2):
            for l in (0, 1):
                mold_wait(l, k, 1, j)

    def weight(l, half):
        total = jnp.zeros((256, 256), F32)
        for p in range(4):
            for cc in (0, 1):
                total += lax.dot_general(
                    acts[l][p, cc].reshape(256, ROWS),
                    molds[l][p, cc, :, 256 * half : 256 * half + 256],
                    NN,
                    preferred_element_type=F32,
                )
        total = total.reshape(4, 64, 256)
        prod[l, half] = total
        wsend[l, half] = total.astype(BF16)

    def weight_copy(l, half, k, src, slot):
        i = (l * 2 + half) * 3 + k - 1
        dst = wrecv.at[l, half, slot]
        return remote(src, dst, w_ss.at[i], w_rs.at[i], line_peer[1 - l](k, c))

    for half in (0, 1):
        for l in (0, 1):
            weight(l, half)
            here = line_at[1 - l]
            for k in (2, 1, 3):
                src = wsend.at[l, half, wrap(here + k, 4)]
                cp = weight_copy(l, half, k, src, here)
                cp.start()
                sent.append(cp)

    back_far(3)

    for half in (0, 1):
        for l in (0, 1):
            for k in (1, 3, 2):
                slot = wrap(line_at[1 - l] - k, 4)
                weight_copy(l, half, k, wrecv.at[l, half, slot], slot).wait_recv()

    def gather_sum(i):
        rows = pl.ds(pl.multiple_of(i * 16, 16), 16)
        for half in (0, 1):
            cols = slice(256 * half, 256 * half + 256)
            lines = []
            for l in (0, 1):
                total = prod[l, half, line_at[1 - l], rows, :]
                for k in (1, 2, 3):
                    total += wrecv[l, half, wrap(line_at[1 - l] - k, 4), rows, :].astype(F32)
                lines.append(total)
            for o in (0, 1):
                both = jnp.concatenate([total[8 * o : 8 * o + 8, :] for total in lines], axis=0)
                zown[2 * i + o, :, cols] = both
                zsend[2 * i + o, :, cols] = both.astype(BF16)

    loop(4, gather_sum)
    for k in (4, 3, 5, 2, 6, 1, 7):
        src = zsend.at[wrap(z + k, 8)]
        send(src, zrecv.at[z], z_ss.at[k - 1], z_rs.at[k - 1], zpeer[k - 1])
    total = zown[z]
    for k in range(1, 8):
        at = zrecv.at[wrap(z - k, 8)]
        remote(at, at, z_ss.at[k - 1], z_rs.at[k - 1], sib).wait_recv()
        total += zrecv[wrap(z - k, 8)].astype(F32)
    gath[n] = total.astype(BF16)
    for k in (6, 2, 5, 7, 1, 3, 4):
        dev = (w, lax.rem(n + k, 8))
        send(gath.at[n], gath.at[n], g_ss.at[k - 1], g_rs.at[k - 1], dev)

    back_close()
    for k in range(1, 8):
        at = gath.at[lax.rem(n - k + 8, 8)]
        remote(at, at, g_ss.at[k - 1], g_rs.at[k - 1], sib).wait_recv()
    for i in range(8):
        total = gath[i].astype(F32)
        weight_out[8 * i : 8 * i + 8, : D // 2] = total[0:8, :]
        weight_out[8 * i : 8 * i + 8, D // 2 :] = total[8:16, :]
    for cp in sent:
        cp.wait_send()


def local(
    compound_activation,
    compound_vectors,
    pathway_vectors,
    matching_pathway_index,
    exponent_of_sharpness,
    offset_shift,
    objective_seed,
):
    vmem = pl.BlockSpec(memory_space=pltpu.VMEM)
    hbm = pl.BlockSpec(memory_space=pltpu.HBM)
    smem = pl.BlockSpec(memory_space=pltpu.SMEM)
    dma = pltpu.SemaphoreType.DMA
    weight_grad, route_grad = pl.pallas_call(
        kernel,
        out_shape=(
            pltpu.VMEM((64, D), F32),
            pltpu.VMEM((ROWS, D), BF16),
        ),
        in_specs=[hbm] * 3 + [vmem] + [smem] * 3,
        out_specs=(vmem, vmem),
        scratch_shapes=[
            pltpu.VMEM((ROWS, FF), BF16),
            pltpu.VMEM((ROWS, D), BF16),
            pltpu.VMEM((ROWS, D), BF16),
            pltpu.VMEM((8, ROWS, D), BF16),
            pltpu.VMEM((4 * ROWS, D), BF16),
            pltpu.VMEM((4, 1, 256), F32),
            pltpu.VMEM((4 * ROWS, 128), F32),
            pltpu.VMEM((4 * ROWS, D), F32),
            pltpu.VMEM((8, ROWS, D), F32),
            pltpu.VMEM((2, 4, ROWS, D), BF16),
            pltpu.VMEM((2, 4, ROWS, D), BF16),
            pltpu.VMEM((8, 1, 256), F32),
            pltpu.VMEM((8, 1, 256), F32),
            pltpu.VMEM((2, ROWS, D), F32),
            pltpu.VMEM((ROWS, D), BF16),
            pltpu.VMEM((ROWS, D), BF16),
            pltpu.VMEM((3, 8, ROWS), F32),
            pltpu.VMEM((3, 8, ROWS), F32),
            pltpu.VMEM((FF, ROWS), F32),
            pltpu.VMEM((2, 4, 4, 64, ROWS), BF16),
            pltpu.VMEM((4, 2, 4, 64, ROWS), BF16),
            pltpu.VMEM((4, 2, 4, 64, ROWS), BF16),
            pltpu.VMEM((4, 2, ROWS, D // 2), BF16),
            pltpu.VMEM((4, 2, ROWS, D // 2), BF16),
            pltpu.VMEM((2, 2, 4, 64, D // 4), F32),
            pltpu.VMEM((2, 2, 4, 64, D // 4), BF16),
            pltpu.VMEM((2, 2, 4, 64, D // 4), BF16),
            pltpu.VMEM((8, 16, D // 2), F32),
            pltpu.VMEM((8, 16, D // 2), BF16),
            pltpu.VMEM((8, 16, D // 2), BF16),
            pltpu.VMEM((8, 16, D // 2), BF16),
            dma((32,)),
            dma((32,)),
            dma((16,)),
            dma((16,)),
            dma((7,)),
            dma((7,)),
            dma((3,)),
            dma((3,)),
            dma((3,)),
            dma((3,)),
            dma((12,)),
            dma((12,)),
            dma((5,)),
            dma((16,)),
            dma((16,)),
            dma((48,)),
            dma((48,)),
            dma((12,)),
            dma((12,)),
            dma((7,)),
            dma((7,)),
            dma((7,)),
            dma((7,)),
        ],
        compiler_params=pltpu.CompilerParams(
            collective_id=0, has_side_effects=True, vmem_limit_bytes=60 * 1024 * 1024
        ),
        name="contrastive_backward",
    )(
        compound_activation[0],
        compound_vectors[0],
        pathway_vectors[0],
        matching_pathway_index,
        exponent_of_sharpness,
        offset_shift,
        objective_seed,
    )
    return weight_grad, route_grad[None]


def solution(mesh):
    in_specs = (
        P("narrow", "wide", None),
        P("narrow", "wide", None),
        P("narrow", "wide", None),
        P("narrow", "wide"),
        P(),
        P(),
        P(),
    )
    out_specs = (P("wide", None), P("narrow", "wide", None))
    return jax.shard_map(local, mesh=mesh, in_specs=in_specs, out_specs=out_specs, check_vma=False)
```

```python
import jax
import jax.numpy as jnp
from jax import lax
from jax.experimental import pallas as pl
from jax.experimental.pallas import tpu as pltpu
from jax.sharding import PartitionSpec as P

ROWS = 160
PIECES = ((0, 48), (48, 32), (80, 48), (128, 32))
CHUNKS = ((0, 32), (32, 64), (96, 32), (128, 32))
D = 1024
FF = 2048
HALF = 80
F32 = jnp.float32
BF16 = jnp.bfloat16
MESH = pl.DeviceIdType.MESH
NT = (((1,), (1,)), ((), ()))
NN = (((1,), (0,)), ((), ()))
TN = (((0,), (0,)), ((), ()))


def wide_of(y, z, c):
    return y * 16 + z * 2 + c


def wrap(i, n):
    return lax.rem(i + n, n)


def loop(n, body):
    lax.fori_loop(0, n, lambda i, _: (body(i), 0)[1], 0)


def kernel(
    act_hbm,
    mol_hbm,
    route_hbm,
    target_ref,
    sharp_ref,
    shift_ref,
    seed_ref,
    weight_out,
    route_out,
    act_ref,
    mol_ref,
    route_ref,
    ring_r,
    cross_m,
    tcross,
    tcol,
    part_m,
    part_r,
    back_out,
    back_in,
    back_along,
    along_in,
    sib_in,
    y_out,
    y_in,
    a_out,
    a_in,
    act_t,
    act_own,
    act_x,
    act_y,
    mold_x,
    mold_y,
    prod,
    wsend,
    wrecv,
    zown,
    zsend,
    zrecv,
    gath,
    ring_ss,
    ring_rs,
    back_ss,
    back_rs,
    along_ss,
    along_rs,
    cross_ss,
    cross_rs,
    t_ss,
    t_rs,
    red_ss,
    red_rs,
    in_s,
    act_ss,
    act_rs,
    mold_ss,
    mold_rs,
    w_ss,
    w_rs,
    z_ss,
    z_rs,
    g_ss,
    g_rs,
):
    w = lax.axis_index("wide")
    n = lax.axis_index("narrow")
    y = lax.div(w, 16)
    z = lax.rem(lax.div(w, 2), 8)
    c = lax.rem(w, 2)
    q = 2 * y + c
    sib = (wide_of(y, z, 1 - c), n)
    across = (wide_of(1 - y, z, c), n)
    diag = (wide_of(1 - y, z, 1 - c), n)
    zpeer = [(wide_of(y, wrap(z + k, 8), c), n) for k in range(1, 8)]

    x = lax.rem(n, 4)
    yh = lax.div(n, 4)
    v = 2 * y + yh

    def x_peer(k, cc):
        return (wide_of(y, z, cc), yh * 4 + wrap(x + k, 4))

    def y_peer(k, cc):
        far = wrap(v + k, 4)
        return (wide_of(lax.div(far, 2), z, cc), lax.rem(far, 2) * 4 + x)

    line_peer = (x_peer, y_peer)
    line_at = (x, v)

    loads = [
        pltpu.make_async_copy(src, dst, in_s.at[i])
        for i, (src, dst) in enumerate(
            ((route_hbm, route_ref), (mol_hbm, mol_ref), (act_hbm, act_ref))
        )
    ]
    for cp in loads:
        cp.start()

    barrier = pltpu.get_barrier_semaphore()
    partners = zpeer + [sib]
    for peer in line_peer:
        partners += [peer(k, cc) for k in (1, 2, 3) for cc in (c, 1 - c)]
    for k in (1, 2, 3):
        partners.append((w, (1 - yh) * 4 + wrap(x + k, 4)))
    for dev in partners:
        pl.semaphore_signal(barrier, inc=1, device_id=dev, device_id_type=MESH)

    sent = []

    def remote(src, dst, ss, rs, dev):
        return pltpu.make_async_remote_copy(
            src_ref=src, dst_ref=dst, send_sem=ss, recv_sem=rs, device_id=dev, device_id_type=MESH
        )

    def send(*a):
        cp = remote(*a)
        cp.start()
        sent.append(cp)

    def block(q_):
        return pl.ds(pl.multiple_of(q_ * ROWS, ROWS), ROWS)

    def unit_rows(raw, rows):
        v = raw[rows, :].astype(F32)
        inv = 1.0 / jnp.sqrt(jnp.sum(v * v, -1, keepdims=True) + 1e-06)
        return v * inv, inv

    def normalise(raw, put):
        def body(i):
            rows = pl.ds(pl.multiple_of(i * 32, 32), 32)
            put(i, rows, unit_rows(raw, rows)[0].astype(BF16))

        loop(ROWS // 32, body)

    def put_ring(i, rows, u):
        ring_r[z, rows, :] = u

    def put_cross(i, rows, u):
        cross_m[pl.ds(pl.multiple_of(q * ROWS + i * 32, 32), 32), :] = u

    loads[0].wait()
    normalise(route_ref, put_ring)
    tcross[q] = jnp.concatenate(
        [target_ref[...].astype(F32), jnp.zeros((1, 256 - ROWS), F32)], axis=1
    )

    pl.semaphore_wait(barrier, len(partners))

    def exists(d, k, h):
        return k < 3 or (k == 3 and h // 2 == d)

    def ring_copy(d, k, h, slot):
        i = (d * 4 + k) * 4 + h
        part = ring_r.at[slot, pl.ds(*PIECES[h])]
        dev = zpeer[0] if d == 0 else zpeer[6]
        return remote(part, part, ring_ss.at[i], ring_rs.at[i], dev)

    def ring_send(d, k, h):
        cp = ring_copy(d, k, h, wrap(z - k, 8) if d == 0 else wrap(z + k, 8))
        cp.start()
        sent.append(cp)

    def ring_wait(d, k, h):
        ring_copy(d, k, h, wrap(z - 1 - k, 8) if d == 0 else wrap(z + 1 + k, 8)).wait_recv()

    order_of = ((0, 1, 2, 3), (2, 3, 0, 1))

    def advance(k, places=(0, 1, 2, 3)):
        for o in places:
            for d in (0, 1):
                h = order_of[d][o]
                if exists(d, k, h):
                    ring_wait(d, k, h)
                    if exists(d, k + 1, h):
                        ring_send(d, k + 1, h)

    def ring_open():
        for o in range(4):
            for d in (0, 1):
                ring_send(d, 0, order_of[d][o])

    b_own, b_sib = block(q), block(2 * y + 1 - c)
    b_across, b_diag = block(2 * (1 - y) + c), block(2 * (1 - y) + 1 - c)

    def cross_copy(i, blk, dev):
        part = cross_m.at[blk]
        return remote(part, part, cross_ss.at[i], cross_rs.at[i], dev)

    def cross_send(i):
        cp = cross_copy(i, b_across if i == 2 else b_own, across if i == 0 else sib)
        cp.start()
        sent.append(cp)

    def cross_wait(i):
        cross_copy(i, (b_across, b_sib, b_diag)[i], sib).wait_recv()

    ring_open()
    loads[1].wait()
    normalise(mol_ref, put_cross)
    cross_send(0)
    for i, dev in enumerate((across, sib, diag)):
        send(tcross.at[q], tcross.at[q], t_ss.at[i], t_rs.at[i], dev)
    cross_send(1)

    loads[2].wait()
    for t in range(16):
        tile = act_ref[:, 128 * t : 128 * t + 128].astype(F32)
        act_t[128 * t : 128 * t + 128, :] = tile.T

    def order(j):
        vv, xx = lax.div(j, 4), lax.rem(j, 4)
        yy, nn = lax.div(vv, 2), lax.rem(vv, 2) * 4 + xx
        for h in (0, 1):
            rows = [
                act_t[pl.ds(pl.multiple_of(1024 * yy + 128 * zz + 64 * h + 8 * nn, 8), 8), :]
                for zz in range(8)
            ]
            act_own[h, vv, xx] = jnp.concatenate(rows, axis=0).astype(BF16)

    loop(16, order)

    acts = (act_x, act_y)
    molds = (mold_x, mold_y)

    def act_part(l, h, at):
        return act_own.at[h, :, at] if l == 0 else act_own.at[h, at]

    own_acts = [
        pltpu.make_async_copy(act_part(l, c, line_at[l]), acts[l].at[line_at[l], c], in_s.at[3 + l])
        for l in (0, 1)
    ]
    for cp in own_acts:
        cp.start()

    def act_send(l):
        here = acts[l].at[line_at[l], c]
        for k in range(4):
            for o in (0, 1):
                if k + o > 0:
                    i = l * 8 + k * 2 + o
                    cc = c if o == 0 else 1 - c
                    src = act_part(l, cc, wrap(line_at[l] + k, 4))
                    send(src, here, act_ss.at[i], act_rs.at[i], line_peer[l](k, cc))

    def act_wait():
        for cp in own_acts:
            cp.wait()
        for l in (0, 1):
            for k in range(4):
                for o in (0, 1):
                    if k + o > 0:
                        i = l * 8 + k * 2 + o
                        cc = c if o == 0 else 1 - c
                        dst = acts[l].at[wrap(line_at[l] - k, 4), cc]
                        remote(dst, dst, act_ss.at[i], act_rs.at[i], sib).wait_recv()

    def mold_copy(l, k, o, j, p, cc, dev):
        i = ((l * 4 + k) * 2 + o) * 4 + j
        at = molds[l].at[p, cc, pl.ds(*CHUNKS[j])]
        return remote(at, at, mold_ss.at[i], mold_rs.at[i], dev)

    def mold_send(l, k, o, j):
        if o == 0:
            cp = mold_copy(l, k, o, j, line_at[l], c, line_peer[l](k, c))
        else:
            cp = mold_copy(l, k, o, j, wrap(line_at[l] - k, 4), c, sib)
        cp.start()
        sent.append(cp)

    def mold_wait(l, k, o, j):
        cc = c if o == 0 else 1 - c
        mold_copy(l, k, o, j, wrap(line_at[l] - k, 4), cc, sib).wait_recv()

    def mold_round(j):
        for k in (2, 1, 3):
            for l in (0, 1):
                mold_send(l, k, 0, j)
        for l in (0, 1):
            mold_send(l, 0, 1, j)

    def mold_pass(j):
        for k in (1, 3, 2):
            for l in (0, 1):
                mold_wait(l, k, 0, j)
                mold_send(l, k, 1, j)

    advance(0)
    cross_wait(0)
    cross_send(2)

    for i, slot in enumerate((2 * (1 - y) + c, 2 * y + 1 - c, 2 * (1 - y) + 1 - c)):
        remote(
            tcross.at[slot], tcross.at[slot], t_ss.at[i], t_rs.at[i], sib
        ).wait_recv()
    eye = lax.broadcasted_iota(jnp.int32, (ROWS, ROWS), 0) == lax.broadcasted_iota(
        jnp.int32, (ROWS, ROWS), 1
    )
    for i in range(4):
        line = jnp.broadcast_to(tcross[i, 0:1, 0:ROWS], (ROWS, ROWS))
        col = jnp.sum(jnp.where(eye, line, 0.0), -1, keepdims=True)
        tcol[i * ROWS : (i + 1) * ROWS, :] = jnp.broadcast_to(col, (ROWS, 128))

    cross_wait(1)
    cross_wait(2)

    shift = shift_ref[0]
    seed = seed_ref[0]

    def pairs(k, first=False, between=None):
        slot = wrap(z + k, 8)
        right = ring_r[slot]
        sharp = jnp.exp(jnp.full((1, ROWS), sharp_ref[0], F32))
        ids = lax.broadcasted_iota(jnp.int32, (1, ROWS), 1) + wide_of(y, slot, c) * ROWS
        ids = ids.astype(F32)
        blocks = [pl.ds(i * ROWS, ROWS) for i in range(4)]

        def grads(b, s):
            match = tcol[b, 0:1] == ids
            g = jax.nn.sigmoid(s * sharp + shift) - jnp.where(match, 1.0, 0.0)
            return (seed * g).astype(BF16)

        scores = [
            lax.dot_general(cross_m[b, :], right, NT, preferred_element_type=F32) for b in blocks
        ]
        gs = [grads(b, s) for b, s in zip(blocks, scores)]
        for b, g in zip(blocks, gs):
            out = lax.dot_general(g, right, NN, preferred_element_type=F32)
            if first:
                part_m[b, :] = out
            else:
                part_m[b, :] += out
        if between is not None:
            between()
        part_r[slot] = lax.dot_general(
            jnp.concatenate(gs, axis=0), cross_m[...], TN, preferred_element_type=F32
        )

    def back_copy(d, s, h):
        rows = pl.ds(h * HALF, HALF)
        i = (d * 4 + s) * 2 + h
        dev = zpeer[0] if d == 0 else zpeer[6]
        return remote(
            back_out.at[d, s, rows], back_in.at[d, s, rows], back_ss.at[i], back_rs.at[i], dev
        )

    def back_send(d, s, h):
        far = h == d
        k = 4 - s if d == 0 else 4 + s
        goal = wrap(z + k, 8)
        carried = s >= (1 if far else 2)
        if carried:
            back_copy(d, s - 1, h).wait_recv()
        spread = jnp.zeros((1, 256), F32)
        for first in range(h * HALF, h * HALF + HALF, 16):
            rows = pl.ds(first, 16)
            total = part_r[goal, rows, :]
            if carried:
                total += back_in[d, s - 1, rows, :].astype(F32)
            unit = ring_r[goal, rows, :].astype(F32)
            along = jnp.sum(total * unit, -1, keepdims=True)
            back_out[d, s, rows, :] = (total - along * unit).astype(BF16)
            place = lax.broadcasted_iota(jnp.int32, (16, 256), 0) + first
            place = place == lax.broadcasted_iota(jnp.int32, (16, 256), 1)
            spread += jnp.sum(jnp.where(place, along, 0.0), 0, keepdims=True)
        cp = back_copy(d, s, h)
        cp.start()
        sent.append(cp)
        if (d == 0) if s == 0 else not far:
            back_along[goal] = spread
        else:
            back_along[goal] += spread
            send(
                back_along.at[goal],
                along_in.at[z],
                along_ss.at[k - 1],
                along_rs.at[k - 1],
                zpeer[k - 1],
            )

    def back_near(s):
        back_send(0, s, 1)
        back_send(1, s, 0)

    def back_far(s):
        back_send(0, s, 0)
        back_send(1, s, 1)

    def back_close():
        for h in (1, 0):
            back_copy(0, 3, h).wait_recv()
            back_copy(1, 3, 1 - h).wait_recv()
        line = jnp.zeros((1, 256), F32)
        for k in range(1, 8):
            at = along_in.at[wrap(z - k, 8)]
            remote(at, at, along_ss.at[k - 1], along_rs.at[k - 1], sib).wait_recv()
            line += along_in[wrap(z - k, 8)]

        def body(i):
            rows = pl.ds(pl.multiple_of(i * 32, 32), 32)
            total = part_r[z, rows, :]
            for d in (0, 1):
                total += back_in[d, 3, rows, :].astype(F32)
            along = jnp.sum(jnp.where(diagonal(i), line[:, :ROWS], 0.0), -1, keepdims=True)
            total += along * ring_r[z, rows, :].astype(F32)
            route_out[rows, :] = norm_back(route_ref, rows, total)

        loop(ROWS // 32, body)

    def reduce_copy(i, j):
        rows = pl.ds(*CHUNKS[j])
        dev = sib
        if i < 2:
            q_ = 2 * (1 - y) + 1 - c if i == 0 else 2 * y + 1 - c
            here = pl.ds(pl.multiple_of(q_ * ROWS + CHUNKS[j][0], 32), CHUNKS[j][1])
            src, dst = part_m.at[here], sib_in.at[i, rows]
        elif i == 2:
            src, dst, dev = y_out.at[rows], y_in.at[rows], across
        else:
            src, dst, dev = a_out.at[j], a_in.at[j], across
        i = i * 4 + j
        return remote(src, dst, red_ss.at[i], red_rs.at[i], dev)

    def reduce_send(i, j):
        cp = reduce_copy(i, j)
        cp.start()
        sent.append(cp)

    def reduce_open():
        for i in (0, 1):
            for j in (0, 1, 2, 3):
                reduce_send(i, j)

    def diagonal(i):
        row = lax.broadcasted_iota(jnp.int32, (32, ROWS), 0) + i * 32
        return row == lax.broadcasted_iota(jnp.int32, (32, ROWS), 1)

    def norm_back(raw, rows, total):
        unit, inv = unit_rows(raw, rows)
        sharp = jnp.exp(jnp.full((32, 1), sharp_ref[0], F32))
        along = jnp.sum(unit * total, -1, keepdims=True)
        return ((total - unit * along) * (inv * sharp)).astype(BF16)

    def blocks_of(j, body):
        first, size = CHUNKS[j]
        loop(size // 32, lambda i: body(i + first // 32))

    def reduce_across(j):
        a_out[j] = jnp.zeros((8, ROWS), F32)
        reduce_copy(0, j).wait_recv()

        def body(i):
            rows = pl.ds(pl.multiple_of(i * 32, 32), 32)
            far = pl.ds(pl.multiple_of((2 * (1 - y) + c) * ROWS + i * 32, 32), 32)
            total = part_m[far, :] + sib_in[0, rows, :]
            unit = cross_m[far, :].astype(F32)
            along = jnp.sum(total * unit, -1, keepdims=True)
            y_out[rows, :] = (total - along * unit).astype(BF16)
            spread = jnp.sum(jnp.where(diagonal(i), along, 0.0), 0, keepdims=True)
            a_out[j] += jnp.broadcast_to(spread, (8, ROWS))

        blocks_of(j, body)
        reduce_send(2, j)
        reduce_send(3, j)

    def reduce_close(j):
        for i in (1, 2, 3):
            reduce_copy(i, j).wait_recv()

        def body(i):
            rows = pl.ds(pl.multiple_of(i * 32, 32), 32)
            own = pl.ds(pl.multiple_of(q * ROWS + i * 32, 32), 32)
            total = part_m[own, :] + sib_in[1, rows, :] + y_in[rows, :].astype(F32)
            along = jnp.sum(jnp.where(diagonal(i), a_in[j, 0:1, :], 0.0), -1, keepdims=True)
            total = total + along * cross_m[own, :].astype(F32)
            value = norm_back(mol_ref, rows, total)
            mold_x[x, c, rows, :] = value[:, : D // 2]
            mold_y[v, c, rows, :] = value[:, D // 2 :]

        blocks_of(j, body)
        mold_round(j)

    act_send(0)
    act_send(1)
    pairs(0, True)
    pairs(-1)
    advance(1, (0, 1))
    pairs(1)
    advance(1, (2, 3))
    pairs(-2)
    advance(2, (0, 1))
    pairs(2)
    advance(2, (2, 3))
    pairs(-3)
    pairs(3)
    back_near(1)
    advance(3)
    pairs(4, between=reduce_open)

    back_far(0)
    reduce_across(0)
    reduce_across(1)
    reduce_across(2)
    reduce_across(3)
    back_near(2)
    reduce_close(0)
    back_far(1)
    reduce_close(1)
    reduce_close(2)
    reduce_close(3)
    back_near(3)
    mold_pass(0)
    back_far(2)
    mold_pass(1)
    mold_pass(2)
    mold_pass(3)
    act_wait()
    for j in (0, 1, 2, 3):
        for k in (0, 1, 3, 2):
            for l in (0, 1):
                mold_wait(l, k, 1, j)

    def weight(l, half):
        total = jnp.zeros((256, 256), F32)
        for p in range(4):
            for cc in (0, 1):
                total += lax.dot_general(
                    acts[l][p, cc].reshape(256, ROWS),
                    molds[l][p, cc, :, 256 * half : 256 * half + 256],
                    NN,
                    preferred_element_type=F32,
                )
        total = total.reshape(4, 64, 256)
        prod[l, half] = total
        wsend[l, half] = total.astype(BF16)

    def weight_copy(l, half, k, src, slot):
        i = (l * 2 + half) * 3 + k - 1
        dst = wrecv.at[l, half, slot]
        return remote(src, dst, w_ss.at[i], w_rs.at[i], line_peer[1 - l](k, c))

    for half in (0, 1):
        for l in (0, 1):
            weight(l, half)
            here = line_at[1 - l]
            for k in (2, 1, 3):
                src = wsend.at[l, half, wrap(here + k, 4)]
                cp = weight_copy(l, half, k, src, here)
                cp.start()
                sent.append(cp)

    back_far(3)

    for half in (0, 1):
        for l in (0, 1):
            for k in (1, 3, 2):
                slot = wrap(line_at[1 - l] - k, 4)
                weight_copy(l, half, k, wrecv.at[l, half, slot], slot).wait_recv()

    def gather_sum(i):
        rows = pl.ds(pl.multiple_of(i * 16, 16), 16)
        for half in (0, 1):
            cols = slice(256 * half, 256 * half + 256)
            lines = []
            for l in (0, 1):
                total = prod[l, half, line_at[1 - l], rows, :]
                for k in (1, 2, 3):
                    total += wrecv[l, half, wrap(line_at[1 - l] - k, 4), rows, :].astype(F32)
                lines.append(total)
            for o in (0, 1):
                both = jnp.concatenate([total[8 * o : 8 * o + 8, :] for total in lines], axis=0)
                zown[2 * i + o, :, cols] = both
                zsend[2 * i + o, :, cols] = both.astype(BF16)

    loop(4, gather_sum)
    for k in (4, 3, 5, 2, 6, 1, 7):
        src = zsend.at[wrap(z + k, 8)]
        send(src, zrecv.at[z], z_ss.at[k - 1], z_rs.at[k - 1], zpeer[k - 1])
    total = zown[z]
    for k in range(1, 8):
        at = zrecv.at[wrap(z - k, 8)]
        remote(at, at, z_ss.at[k - 1], z_rs.at[k - 1], sib).wait_recv()
        total += zrecv[wrap(z - k, 8)].astype(F32)
    gath[n] = total.astype(BF16)
    for k in (6, 2, 5, 7, 1, 3, 4):
        dev = (w, lax.rem(n + k, 8))
        send(gath.at[n], gath.at[n], g_ss.at[k - 1], g_rs.at[k - 1], dev)

    back_close()
    for k in range(1, 8):
        at = gath.at[lax.rem(n - k + 8, 8)]
        remote(at, at, g_ss.at[k - 1], g_rs.at[k - 1], sib).wait_recv()
    for i in range(8):
        total = gath[i].astype(F32)
        weight_out[8 * i : 8 * i + 8, : D // 2] = total[0:8, :]
        weight_out[8 * i : 8 * i + 8, D // 2 :] = total[8:16, :]
    for cp in sent:
        cp.wait_send()


def local(
    compound_activation,
    compound_vectors,
    pathway_vectors,
    matching_pathway_index,
    exponent_of_sharpness,
    offset_shift,
    objective_seed,
):
    vmem = pl.BlockSpec(memory_space=pltpu.VMEM)
    hbm = pl.BlockSpec(memory_space=pltpu.HBM)
    smem = pl.BlockSpec(memory_space=pltpu.SMEM)
    dma = pltpu.SemaphoreType.DMA
    weight_grad, route_grad = pl.pallas_call(
        kernel,
        out_shape=(
            pltpu.VMEM((64, D), F32),
            pltpu.VMEM((ROWS, D), BF16),
        ),
        in_specs=[hbm] * 3 + [vmem] + [smem] * 3,
        out_specs=(vmem, vmem),
        scratch_shapes=[
            pltpu.VMEM((ROWS, FF), BF16),
            pltpu.VMEM((ROWS, D), BF16),
            pltpu.VMEM((ROWS, D), BF16),
            pltpu.VMEM((8, ROWS, D), BF16),
            pltpu.VMEM((4 * ROWS, D), BF16),
            pltpu.VMEM((4, 1, 256), F32),
            pltpu.VMEM((4 * ROWS, 128), F32),
            pltpu.VMEM((4 * ROWS, D), F32),
            pltpu.VMEM((8, ROWS, D), F32),
            pltpu.VMEM((2, 4, ROWS, D), BF16),
            pltpu.VMEM((2, 4, ROWS, D), BF16),
            pltpu.VMEM((8, 1, 256), F32),
            pltpu.VMEM((8, 1, 256), F32),
            pltpu.VMEM((2, ROWS, D), F32),
            pltpu.VMEM((ROWS, D), BF16),
            pltpu.VMEM((ROWS, D), BF16),
            pltpu.VMEM((4, 8, ROWS), F32),
            pltpu.VMEM((4, 8, ROWS), F32),
            pltpu.VMEM((FF, ROWS), F32),
            pltpu.VMEM((2, 4, 4, 64, ROWS), BF16),
            pltpu.VMEM((4, 2, 4, 64, ROWS), BF16),
            pltpu.VMEM((4, 2, 4, 64, ROWS), BF16),
            pltpu.VMEM((4, 2, ROWS, D // 2), BF16),
            pltpu.VMEM((4, 2, ROWS, D // 2), BF16),
            pltpu.VMEM((2, 2, 4, 64, D // 4), F32),
            pltpu.VMEM((2, 2, 4, 64, D // 4), BF16),
            pltpu.VMEM((2, 2, 4, 64, D // 4), BF16),
            pltpu.VMEM((8, 16, D // 2), F32),
            pltpu.VMEM((8, 16, D // 2), BF16),
            pltpu.VMEM((8, 16, D // 2), BF16),
            pltpu.VMEM((8, 16, D // 2), BF16),
            dma((32,)),
            dma((32,)),
            dma((16,)),
            dma((16,)),
            dma((7,)),
            dma((7,)),
            dma((3,)),
            dma((3,)),
            dma((3,)),
            dma((3,)),
            dma((16,)),
            dma((16,)),
            dma((5,)),
            dma((16,)),
            dma((16,)),
            dma((64,)),
            dma((64,)),
            dma((12,)),
            dma((12,)),
            dma((7,)),
            dma((7,)),
            dma((7,)),
            dma((7,)),
        ],
        compiler_params=pltpu.CompilerParams(
            collective_id=0, has_side_effects=True, vmem_limit_bytes=60 * 1024 * 1024
        ),
        name="contrastive_backward",
    )(
        compound_activation[0],
        compound_vectors[0],
        pathway_vectors[0],
        matching_pathway_index,
        exponent_of_sharpness,
        offset_shift,
        objective_seed,
    )
    return weight_grad, route_grad[None]


def solution(mesh):
    in_specs = (
        P("narrow", "wide", None),
        P("narrow", "wide", None),
        P("narrow", "wide", None),
        P("narrow", "wide"),
        P(),
        P(),
        P(),
    )
    out_specs = (P("wide", None), P("narrow", "wide", None))
    return jax.shard_map(local, mesh=mesh, in_specs=in_specs, out_specs=out_specs, check_vma=False)
```
